256 devices in a mesh: dom: 256 (over x, z, y, core).
Axes of the slice: x: 4, y: 4, z: 8, core: 2. Of those that a mesh axis runs over, the one named last changes fastest.
Arguments:
- stress: float32 [6, 786432], P(None, 'dom'), may hold values from -6 to 6
- stress_dir: float32 [6, 786432], P(None, 'dom'), may hold values from -6 to 6
- adjoint: float32 [6, 786432], P(None, 'dom'), may hold values from -6 to 6
- relax: float32 [786432], P('dom'), may hold values from 0.2 to 2
- relax_dir: float32 [786432], P('dom'), may hold values from -6 to 6
- connect: int32 [4, 4194304], P(None, 'dom'), may hold values from 0 to 5119, as said below
- mass_mat: float32 [16, 4194304], P(None, 'dom'), may hold values from 0.02 to 0.1
- adv_mat: float32 [16, 4194304], P(None, 'dom'), may hold values from -0.6 to 0.6
- vel_grad: float32 [9, 4194304], P(None, 'dom'), may hold values from -3 to 3
- send_list: int32 [524288], P('dom'), may hold values from -1 to 3071, as said below
- elem_count: int32 [256], P('dom'), may hold values from 4096 to 16384, as said below
Outputs:
- inc_residual: float32 [6, 786432], P(None, 'dom')
- hess_action: float32 [786432], P('dom')
The draws below stay inside these ranges and needn't reach their ends.
Inputs may be any that keep to these rules, and one draw needn't show every extreme that they name: `connect`: each device's entries are below 5120; an entry at or above 3072 names a ghost slot that holds a node. In element block b (slots b * 512 to (b + 1) * 512 - 1) an owned entry lies in start_b to start_b + 383 with start_b = (b * 2688) // max(31, 1), and a ghost entry lies in list b % 16. `send_list`: in each list the live entries (owned node indices) come first, the rest are -1; a list to a neighbour off the ends of the axis is all -1; every partition has a list with all 128 slots live. `elem_count`: some partition has all 16384 slots live and another has 4096.
All inputs are finite; a program needn't handle non-finite values.
Results may differ from the reference program's by a relative error of at most 0.0003.
Values sent between devices are 32-bit elements; how exact they have to be, the bound alone decides.
A program may use at most 64 MiB of HBM per device.

```python
import math
import jax
import jax.numpy as jnp
from jax import lax

NODE_DEV = 3072
ELEM_DEV = 16384
GHOST_CAP = 128
HOPS = 8
ELEM_BLOCK = 512
WINDOW = 384
NODES = 786432
ELEMS = 4194304
N_DOM = 256


def ghost_counts(key):
    base = jax.random.fold_in(key, 7101)
    first, second = jax.random.split(base)
    counts = jax.random.randint(first, (N_DOM, 2 * HOPS), GHOST_CAP // 4, GHOST_CAP + 1)
    offsets = jnp.concatenate([jnp.arange(1, HOPS + 1), -jnp.arange(1, HOPS + 1)]).astype(jnp.int32)
    parts = jnp.arange(N_DOM, dtype=jnp.int32)[:, None]
    target = parts + offsets[None, :]
    inside = (target >= 0) & (target < N_DOM)
    chosen = jax.random.randint(second, (N_DOM,), 0, HOPS)
    up_ok = parts[:, 0] + chosen + 1 < N_DOM
    slot = jnp.where(up_ok, chosen, chosen + HOPS)
    full = jnp.arange(2 * HOPS, dtype=jnp.int32)[None, :] == slot[:, None]
    counts = jnp.where(full, GHOST_CAP, counts)
    counts = jnp.where(inside, counts, 0)
    return (counts.astype(jnp.int32), offsets)


def draw_send_list(key, part):
    counts, offsets = ghost_counts(key)
    picks = jax.random.randint(jax.random.fold_in(key, 7202), (N_DOM, 2 * HOPS, GHOST_CAP), 0, NODE_DEV)
    slots = jnp.arange(GHOST_CAP, dtype=jnp.int32)[None, None, :]
    lists = jnp.where(slots < counts[:, :, None], picks, -1)
    return lists.reshape(-1).astype(jnp.int32)


def draw_connect(key, part):
    counts, offsets = ghost_counts(key)
    parts = jnp.arange(N_DOM, dtype=jnp.int32)[:, None]
    source = parts - offsets[None, :]
    inside = (source >= 0) & (source < N_DOM)
    clipped = jnp.clip(source, 0, N_DOM - 1)
    received = jnp.where(inside, counts[clipped, jnp.arange(2 * HOPS, dtype=jnp.int32)[None, :]], 0)
    keys = jax.random.split(jax.random.fold_in(key, 7303), 4)
    shape = (N_DOM, 4, ELEM_DEV)
    nblocks = ELEM_DEV // ELEM_BLOCK
    span = max(nblocks - 1, 1)
    block = jnp.arange(ELEM_DEV, dtype=jnp.int32) // ELEM_BLOCK
    first = block * (NODE_DEV - WINDOW) // span
    region_row = block % (2 * HOPS)
    region = jnp.broadcast_to(region_row[None, None, :], shape)
    owned = first[None, None, :] + jax.random.randint(keys[0], shape, 0, WINDOW)
    coin = jax.random.randint(keys[1], shape, 0, 100)
    avail = jnp.take_along_axis(received[:, None, :], region.reshape(N_DOM, 1, -1), axis=2).reshape(shape)
    raw = jax.random.randint(keys[3], shape, 0, 1 << 20)
    slot = raw % jnp.maximum(avail, 1)
    ghost = NODE_DEV + region * GHOST_CAP + slot
    use_ghost = (coin < 15) & (avail > 0)
    local = jnp.where(use_ghost, ghost, owned)
    return local.transpose(1, 0, 2).reshape(4, N_DOM * ELEM_DEV).astype(jnp.int32)


def draw_elem_count(key, part):
    keys = jax.random.split(jax.random.fold_in(key, 7404), 3)
    counts = jax.random.randint(keys[0], (N_DOM,), ELEM_DEV // 4, ELEM_DEV + 1)
    fullest = jax.random.randint(keys[1], (), 0, N_DOM)
    lightest = (fullest + 1 + jax.random.randint(keys[2], (), 0, N_DOM - 1)) % N_DOM
    index = jnp.arange(N_DOM)
    counts = jnp.where(index == fullest, ELEM_DEV, counts)
    counts = jnp.where(index == lightest, ELEM_DEV // 4, counts)
    return counts.astype(jnp.int32)


def block_scale(key, shape, pieces, least, high):
    def one(position, shards_of):
        steps = jax.random.uniform(jax.random.fold_in(jax.random.fold_in(key, 6), position), (shards_of,), jnp.float32, least / len(pieces), high / len(pieces))
        return jnp.repeat(jnp.exp(steps), shape[position] // shards_of).reshape((-1,) + (1,) * (len(shape) - position - 1))

    loudness = one(*pieces[0])
    for cut in pieces[1:]:
        loudness = loudness * one(*cut)
    return loudness


def noise(own_key, shape, width, limit, cuts=(), held_as=jnp.bfloat16):
    array = jax.random.normal(own_key, shape, jnp.float32) * width
    if len(cuts) > 0:
        array = block_scale(own_key, shape, cuts, -0.22, 0.18) * array
    return jnp.clip(array, min=-limit, max=limit).astype(held_as)


def setup_inputs(seed: int = 0) -> dict:
    key_list = jax.random.split(jax.random.key(seed), 12)
    stress = noise(key_list[0], (6, NODES), 1.0, 6.0, ((1, 256),), jnp.float32)
    stress_dir = noise(key_list[1], (6, NODES), 1.0, 6.0, ((1, 256),), jnp.float32)
    adjoint = noise(key_list[2], (6, NODES), 1.0, 6.0, ((1, 256),), jnp.float32)
    relax = jnp.clip(jnp.exp(math.log(2.0) - 2.3025851 * jax.random.uniform(key_list[3], (NODES,), jnp.float32) ** block_scale(key_list[3], (NODES,), ((0, 256),), -0.2, 0.2)), 0.2, 2.0)
    relax_dir = noise(key_list[4], (NODES,), 1.0, 6.0, ((0, 256),), jnp.float32)
    connect = draw_connect(jax.random.fold_in(key_list[11], 71), 0)
    mass_mat = jnp.clip(0.02 + 0.08 * jax.random.uniform(key_list[6], (16, ELEMS), jnp.float32) ** block_scale(key_list[6], (16, ELEMS), ((1, 256),), -0.2, 0.2), 0.02, 0.1)
    adv_mat = noise(key_list[7], (16, ELEMS), 0.1, 0.6, ((1, 256),), jnp.float32)
    vel_grad = noise(key_list[8], (9, ELEMS), 0.5, 3.0, ((1, 256),), jnp.float32)
    send_list = draw_send_list(jax.random.fold_in(key_list[11], 71), 0)
    elem_count = draw_elem_count(jax.random.fold_in(key_list[11], 71), 0)
    return {"stress": stress, "stress_dir": stress_dir, "adjoint": adjoint, "relax": relax, "relax_dir": relax_dir, "connect": connect, "mass_mat": mass_mat, "adv_mat": adv_mat, "vel_grad": vel_grad, "send_list": send_list, "elem_count": elem_count}


KAPPA = 0.5
PAIRS = ((0, 0), (1, 1), (2, 2), (0, 1), (0, 2), (1, 2))
LAYOUT = ((0, 3, 4), (3, 1, 5), (4, 5, 2))


def full_tensor(comps):
    return [[comps[LAYOUT[row][col]] for col in range(3)] for row in range(3)]


def convect(grad, comps):
    tensor = full_tensor(comps)
    result = []
    for row, col in PAIRS:
        total = jnp.zeros_like(comps[0])
        for inner in range(3):
            total = total + grad[3 * row + inner] * tensor[inner][col] + tensor[row][inner] * grad[3 * col + inner]
        result.append(total)
    return jnp.stack(result)


def pair_product(first, second):
    left = full_tensor(first)
    right = full_tensor(second)
    result = []
    for row, col in PAIRS:
        total = jnp.zeros_like(first[0])
        for inner in range(3):
            total = total + left[row][inner] * right[inner][col] + right[row][inner] * left[inner][col]
        result.append(total)
    return jnp.stack(result)


def apply_matrix(matrix, field):
    rows_out = []
    for first in range(4):
        total = jnp.zeros_like(field[:, 0])
        for second in range(4):
            total = total + matrix[4 * first + second] * field[:, second]
        rows_out.append(total)
    return jnp.stack(rows_out, axis=1)


def element_terms(values, mass, advect, grad, live):
    tau = values[0:6]
    tdir = values[6:12]
    adj = values[12:18]
    lam_e = jnp.mean(values[18], axis=0)
    dlam_e = jnp.mean(values[19], axis=0)
    gterm = apply_matrix(advect, tdir) - apply_matrix(mass, convect(grad, tdir)) + KAPPA * apply_matrix(mass, pair_product(tau, tdir))
    bterm = apply_matrix(advect, tau) - apply_matrix(mass, convect(grad, tau)) + 0.5 * KAPPA * apply_matrix(mass, pair_product(tau, tau))
    dres = apply_matrix(mass, tdir) + lam_e * gterm + dlam_e * bterm
    score = 0.25 * jnp.sum(adj * gterm, axis=(0, 1))
    hterm = jnp.broadcast_to(score, dres.shape[1:])[None]
    weight = live.astype(jnp.float32)
    return jnp.concatenate([dres, hterm], axis=0) * weight


def reference(stress, stress_dir, adjoint, relax, relax_dir, connect, mass_mat, adv_mat, vel_grad, send_list, elem_count):
    ndev = N_DOM
    node_dev = NODE_DEV
    elem_dev = ELEM_DEV
    fields = jnp.concatenate([stress, stress_dir, adjoint, relax[None], relax_dir[None]], axis=0)
    padded = jnp.concatenate([fields, jnp.zeros((20, 1), jnp.float32)], axis=1)
    offsets = jnp.concatenate([jnp.arange(1, HOPS + 1, dtype=jnp.int32), -jnp.arange(1, HOPS + 1, dtype=jnp.int32)])
    sends = send_list.reshape(ndev, 2 * HOPS, GHOST_CAP)
    parts = jnp.arange(ndev, dtype=jnp.int32)
    source = parts[:, None] - offsets[None, :]
    inside = (source >= 0) & (source < ndev)
    clipped = jnp.clip(source, 0, ndev - 1)
    sent = sends[clipped, jnp.arange(2 * HOPS, dtype=jnp.int32)[None, :], :]
    usable = inside[:, :, None] & (sent >= 0)
    ghost_ids = jnp.where(usable, clipped[:, :, None] * node_dev + sent, ndev * node_dev).astype(jnp.int32)
    own_ids = parts[:, None] * node_dev + jnp.arange(node_dev, dtype=jnp.int32)[None, :]
    global_map = jnp.concatenate([own_ids, ghost_ids.reshape(ndev, -1)], axis=1).astype(jnp.int32)
    conn_dev = connect.reshape(4, ndev, elem_dev).transpose(1, 0, 2)
    mass_dev = mass_mat.reshape(16, ndev, elem_dev).transpose(1, 0, 2)
    adv_dev = adv_mat.reshape(16, ndev, elem_dev).transpose(1, 0, 2)
    grad_dev = vel_grad.reshape(9, ndev, elem_dev).transpose(1, 0, 2)

    def visit(total, inputs):
        gmap, conn, mass, advect, grad, count = inputs
        gid = jnp.take(gmap, conn).astype(jnp.int32)
        values = padded[:, gid]
        live = jnp.arange(elem_dev, dtype=jnp.int32) < count
        terms = element_terms(values, mass, advect, grad, live)
        return total.at[:, gid].add(terms), None

    start = jnp.zeros((7, ndev * node_dev + 1), jnp.float32)
    total, _ = lax.scan(visit, start, (global_map, conn_dev, mass_dev, adv_dev, grad_dev, elem_count))
    return total[0:6, :-1], total[6, :-1]
```

```python
import jax
import jax.numpy as jnp
from jax import lax
from jax.experimental import pallas as pl
from jax.experimental.pallas import tpu as pltpu
from jax.sharding import PartitionSpec as P

HOPS = 8
LISTS = 2 * HOPS
ELEM_BLOCK = 512
KAPPA = 0.5
PAIRS = ((0, 0), (1, 1), (2, 2), (0, 1), (0, 2), (1, 2))
LAYOUT = ((0, 3, 4), (3, 1, 5), (4, 5, 2))

LANES = 128
ROWS = 24
TAU, LAM, DLAM, DIR, ADJ = 0, 6, 7, 8, 16
FIELD_ROWS = tuple(range(0, 14)) + tuple(range(16, 22))
WIN = 3
TERM = 8

GATHER = lax.GatherDimensionNumbers(
    offset_dims=(),
    collapsed_slice_dims=(1,),
    start_index_map=(1,),
    operand_batching_dims=(0,),
    start_indices_batching_dims=(0,),
)


def pick_lanes(table, lane):
    return lax.gather(
        table,
        lane[:, :, None],
        GATHER,
        slice_sizes=(1, 1),
        mode=lax.GatherScatterMode.PROMISE_IN_BOUNDS,
    )


def list_offset(index):
    return jnp.where(index < HOPS, index + 1, HOPS - 1 - index)


def row_of(ref, row, height=8):
    return jnp.broadcast_to(ref[pl.ds(row, 1), :], (height, LANES))


def two_parts(values):
    high = values.astype(jnp.bfloat16)
    low = (values - high.astype(jnp.float32)).astype(jnp.bfloat16)
    return jnp.concatenate([high, low], axis=0)


def symmetric_product(left, right):
    prod = [
        [
            left[row][0] * right[LAYOUT[0][col]]
            + left[row][1] * right[LAYOUT[1][col]]
            + left[row][2] * right[LAYOUT[2][col]]
            for col in range(3)
        ]
        for row in range(3)
    ]
    return [prod[row][col] + prod[col][row] for row, col in PAIRS]


def make_kernel(ndev, nodes, elems):
    chunks = nodes // LANES
    nblocks = elems // ELEM_BLOCK
    groups = ELEM_BLOCK // LANES
    steps = nblocks // 2
    span = max(nblocks - 1, 1)
    window = WIN * LANES

    def kernel(
        stress_hbm,
        dir_hbm,
        adj_hbm,
        relax_hbm,
        rdir_hbm,
        conn_hbm,
        mass_hbm,
        adv_hbm,
        grad_hbm,
        send_hbm,
        count_ref,
        res_hbm,
        hess_hbm,
        stress,
        sdir,
        adjoint,
        relax,
        rdir,
        conn,
        mass,
        adv,
        grad,
        send,
        res,
        hess,
        fields,
        payload,
        ghosts,
        rolled,
        values,
        gradv,
        grad8,
        index_rows,
        terms,
        acc,
        gout,
        returned,
        in_sem,
        out_sem,
        send_sem,
        recv_sem,
        back_sem,
        ret_sem,
    ):
        me = lax.axis_index("dom")
        loads = [
            pltpu.make_async_copy(src, dst, in_sem.at[i])
            for i, (src, dst) in enumerate(
                [
                    (stress_hbm, stress),
                    (dir_hbm, sdir),
                    (adj_hbm, adjoint),
                    (relax_hbm, relax),
                    (rdir_hbm, rdir),
                    (send_hbm, send),
                    (conn_hbm, conn),
                    (grad_hbm, grad),
                    (mass_hbm, mass),
                    (adv_hbm, adv),
                ]
            )
        ]
        for load in loads:
            load.start()

        def inside(device):
            return (device >= 0) & (device < ndev)

        barrier = pltpu.get_barrier_semaphore()

        @pl.loop(0, LISTS)
        def _(k):
            target = me + list_offset(k)

            @pl.when(inside(target))
            def _():
                pl.semaphore_signal(
                    barrier, inc=1, device_id=(target,), device_id_type=pl.DeviceIdType.MESH
                )

        zeros = jnp.zeros((8, LANES), jnp.float32)
        lane = lax.broadcasted_iota(jnp.int32, (8, LANES), 1)
        sub = lax.broadcasted_iota(jnp.int32, (8, LANES), 0)
        upper = sub >= groups

        for load in loads[:6]:
            load.wait()

        for c in range(chunks):
            cut = pl.ds(c * LANES, LANES)
            for base in (TAU, DIR, ADJ):
                fields[pl.ds(c * ROWS + base, 8), :] = zeros
            fields[pl.ds(c * ROWS + TAU, 6), :] = stress[:, cut]
            fields[pl.ds(c * ROWS + LAM, 1), :] = relax[pl.ds(c, 1), :]
            fields[pl.ds(c * ROWS + DLAM, 1), :] = rdir[pl.ds(c, 1), :]
            fields[pl.ds(c * ROWS + DIR, 6), :] = sdir[:, cut]
            fields[pl.ds(c * ROWS + ADJ, 6), :] = adjoint[:, cut]
        for base in (TAU, DIR, ADJ):
            fields[pl.ds(chunks * ROWS + base, 8), :] = zeros

        @pl.loop(0, LISTS)
        def _(k):
            entry = row_of(send, k)
            place = entry & (LANES - 1)
            chunk = entry >> 7
            picked = [zeros, zeros, zeros]
            for c in range(chunks):
                here = chunk == c
                for t in range(3):
                    got = pick_lanes(fields[pl.ds(c * ROWS + 8 * t, 8), :], place)
                    picked[t] = jnp.where(here, got, picked[t])
            for t in range(3):
                payload[k, pl.ds(8 * t, 8), :] = picked[t]

        first_up = jnp.minimum(HOPS, ndev - 1 - me)
        first_down = jnp.minimum(HOPS, me)
        pl.semaphore_wait(barrier, first_up + first_down)

        def push(k):
            target = me + list_offset(k)
            return pltpu.make_async_remote_copy(
                src_ref=payload.at[k],
                dst_ref=ghosts.at[k],
                send_sem=send_sem.at[k],
                recv_sem=recv_sem.at[k],
                device_id=(target,),
                device_id_type=pl.DeviceIdType.MESH,
            )

        def push_back(k):
            target = me - list_offset(k)
            return pltpu.make_async_remote_copy(
                src_ref=gout.at[k],
                dst_ref=returned.at[k],
                send_sem=back_sem.at[k],
                recv_sem=ret_sem.at[k],
                device_id=(target,),
                device_id_type=pl.DeviceIdType.MESH,
            )

        @pl.loop(0, LISTS)
        def _(k):
            @pl.when(inside(me + list_offset(k)))
            def _():
                push(k).start()

        for i in range(chunks + 1):
            acc[pl.ds(i * TERM, TERM), :] = zeros
        for i in range(LISTS):
            gout[i] = zeros
        for k in range(4):
            for g in range(8):
                terms[k, pl.ds(g * TERM, TERM), :] = zeros

        for load in loads[6:8]:
            load.wait()

        def starts_of(pair):
            one = (2 * pair) * (nodes - window) // span
            two = (2 * pair + 1) * (nodes - window) // span
            return one, two

        def relative(pair, k):
            one, two = starts_of(pair)
            lists_one = (2 * pair) % LISTS
            node = conn[pl.ds(pair * 32 + k, 8, stride=4), :]
            start = jnp.where(upper, two, one)
            ghost0 = nodes + LANES * jnp.where(upper, lists_one + 1, lists_one) - window
            return node - jnp.where(node >= nodes, ghost0, start)

        @pl.loop(0, steps)
        def _(pair):
            for which, start in enumerate(starts_of(pair)):
                chunk0 = start // LANES
                shift = start % LANES
                keep = lane < LANES - shift
                for t in range(3):
                    turned = [
                        pltpu.roll(
                            fields[
                                pl.ds(pl.multiple_of((chunk0 + i) * ROWS + 8 * t, 8), 8), :
                            ],
                            (LANES - shift) % LANES,
                            1,
                        )
                        for i in range(WIN + 1)
                    ]
                    for i in range(WIN):
                        rolled[which, pl.ds(i * ROWS + 8 * t, 8), :] = jnp.where(
                            keep, turned[i], turned[i + 1]
                        )
            places, firsts, seconds = [], [], []
            for k in range(4):
                rel = relative(pair, k)
                places.append(rel & (LANES - 1))
                firsts.append(rel < LANES)
                seconds.append(rel < 2 * LANES)
            for n, row in enumerate(FIELD_ROWS):
                table = [
                    jnp.where(
                        upper,
                        row_of(rolled.at[1], i * ROWS + row),
                        row_of(rolled.at[0], i * ROWS + row),
                    )
                    for i in range(WIN)
                ]
                for k in range(4):
                    a, b, c = [pick_lanes(table[i], places[k]) for i in range(WIN)]
                    values[pair, k * 20 + n] = jnp.where(
                        firsts[k], a, jnp.where(seconds[k], b, c)
                    )
            for j in range(8):
                cut = pl.ds(pl.multiple_of((pair * 8 + j) * LANES, LANES), LANES)
                gradv[pl.ds(pl.multiple_of((pair * 8 + j) * 8, 8), 8), :] = grad[0:8, cut]
                grad8[pl.ds(pair * 8 + j, 1), :] = grad[8:9, cut]

        for load in loads[8:]:
            load.wait()

        count = count_ref[0]
        columns = lax.broadcasted_iota(jnp.int32, (LANES, LANES), 0).astype(jnp.bfloat16)
        one16 = jnp.ones((LANES, LANES), jnp.bfloat16)
        zero16 = jnp.zeros((LANES, LANES), jnp.bfloat16)
        contract = (((1,), (1,)), ((), ()))

        def factor(place_row):
            return jnp.where(columns == place_row, one16, zero16)

        def visit(pair):
            listed = (2 * pair) % LISTS
            rels = [relative(pair, k) for k in range(4)]
            places = [rel & (LANES - 1) for rel in rels]
            ghostly = [rel >= window for rel in rels]
            got = [[None] * 20 for _ in range(4)]
            for n, row in enumerate(FIELD_ROWS):
                table = jnp.where(
                    upper, row_of(ghosts.at[listed + 1], row), row_of(ghosts.at[listed], row)
                )
                for k in range(4):
                    got[k][n] = jnp.where(
                        ghostly[k], pick_lanes(table, places[k]), values[pair, k * 20 + n]
                    )
            lam_e = 0.25 * (got[0][6] + got[1][6] + got[2][6] + got[3][6])
            dlam_e = 0.25 * (got[0][7] + got[1][7] + got[2][7] + got[3][7])
            vel = [
                gradv[pl.ds(pair * 64 + i, 8, stride=8), :] for i in range(8)
            ] + [grad8[pl.ds(pl.multiple_of(pair * 8, 8), 8), :]]
            tdir, gin, wsum, usum = [], [], [], []
            for k in range(4):
                tau = got[k][0:6]
                t = got[k][8:14]
                half = [KAPPA * s for s in tau]
                quarter = [0.5 * s for s in half]
                left_g = [
                    [half[LAYOUT[r][c]] - vel[3 * r + c] for c in range(3)] for r in range(3)
                ]
                left_b = [
                    [quarter[LAYOUT[r][c]] - vel[3 * r + c] for c in range(3)] for r in range(3)
                ]
                b_in = symmetric_product(left_b, tau)
                tdir.append(t)
                gin.append(symmetric_product(left_g, t))
                wsum.append([dlam_e * s for s in tau])
                usum.append([t[c] + dlam_e * b_in[c] for c in range(6)])
            score = zeros
            for a in range(4):
                mat = [
                    mass[pl.ds(((4 * a + b) // 8) * elems // 16 + pair * 64 + (4 * a + b) % 8, 8, stride=8), :]
                    for b in range(4)
                ]
                adm = [
                    adv[pl.ds(((4 * a + b) // 8) * elems // 16 + pair * 64 + (4 * a + b) % 8, 8, stride=8), :]
                    for b in range(4)
                ]
                for c in range(6):
                    g = adm[0] * tdir[0][c] + mat[0] * gin[0][c]
                    d = adm[0] * wsum[0][c] + mat[0] * usum[0][c]
                    for b in range(1, 4):
                        g = g + (adm[b] * tdir[b][c] + mat[b] * gin[b][c])
                        d = d + (adm[b] * wsum[b][c] + mat[b] * usum[b][c])
                    score = score + got[a][14 + c] * g
                    terms[a, pl.ds(c, 8, stride=TERM), :] = d + lam_e * g
            score = 0.25 * score
            for a in range(4):
                terms[a, pl.ds(6, 8, stride=TERM), :] = score

            live = (pair * 8 + sub) * LANES + lane < count
            for k in range(4):
                index_rows[0, pl.ds(8 * k, 8), :] = places[k].astype(jnp.float32)
                index_rows[1, pl.ds(8 * k, 8), :] = jnp.where(live, rels[k] >> 7, -1).astype(
                    jnp.float32
                )
            for which, start in enumerate(starts_of(pair)):
                total = jnp.zeros((4 * 2 * TERM, LANES), jnp.float32)
                for k in range(4):
                    lefts, rights = [], []
                    for j in range(groups):
                        g = which * groups + j
                        part = two_parts(terms[k, pl.ds(g * TERM, TERM), :])
                        chunk = row_of(index_rows.at[1], 8 * k + g, 16).astype(jnp.bfloat16)
                        place = row_of(index_rows.at[0], 8 * k + g, 16).astype(jnp.bfloat16)
                        lefts.append(
                            jnp.concatenate(
                                [
                                    jnp.where(chunk == float(i), part, zero16[:16])
                                    for i in range(4)
                                ],
                                axis=0,
                            )
                        )
                        rights.append(factor(jnp.concatenate([place] * 8, axis=0)))
                    total = total + lax.dot_general(
                        jnp.concatenate(lefts, axis=1),
                        jnp.concatenate(rights, axis=1),
                        contract,
                        preferred_element_type=jnp.float32,
                    )
                sums = [
                    total[16 * i : 16 * i + 8] + total[16 * i + 8 : 16 * i + 16]
                    for i in range(4)
                ]
                chunk0 = start // LANES
                shift = start % LANES
                turned = [pltpu.roll(sums[i], shift, 1) for i in range(WIN)]
                later = lane >= shift
                for i in range(WIN + 1):
                    if i == 0:
                        add = jnp.where(later, turned[0], 0.0)
                    elif i == WIN:
                        add = jnp.where(later, 0.0, turned[WIN - 1])
                    else:
                        add = jnp.where(later, turned[i], turned[i - 1])
                    at = pl.ds(pl.multiple_of((chunk0 + i) * TERM, TERM), TERM)
                    acc[at, :] = acc[at, :] + add
                gout[listed + which] = gout[listed + which] + sums[WIN]

        turns = LISTS // 2
        rounds = steps // turns

        @pl.loop(0, turns)
        def _(turn):
            for which in range(2):
                k = 2 * turn + which

                @pl.when(inside(me - list_offset(k)))
                def _():
                    push(k).wait_recv()

            @pl.loop(0, rounds)
            def _(r):
                visit(turn + r * turns)

            for which in range(2):
                k = 2 * turn + which

                @pl.when(inside(me - list_offset(k)))
                def _():
                    push_back(k).start()

        @pl.loop(0, LISTS)
        def _(k):
            @pl.when(inside(me + list_offset(k)))
            def _():
                push_back(k).wait_recv()

        total = jnp.zeros((chunks * 2 * TERM, LANES), jnp.float32)
        for pairing in range(LISTS // 2):
            lefts, rights = [], []
            for k in (2 * pairing, 2 * pairing + 1):
                entry = row_of(send, k)
                part = two_parts(jnp.where(entry >= 0, returned[k], 0.0))
                entry16 = row_of(send, k, 16)
                chunk = (entry16 >> 7).astype(jnp.float32).astype(jnp.bfloat16)
                place = (entry16 & (LANES - 1)).astype(jnp.float32).astype(jnp.bfloat16)
                lefts.append(
                    jnp.concatenate(
                        [
                            jnp.where(chunk == float(i), part, zero16[:16])
                            for i in range(chunks)
                        ],
                        axis=0,
                    )
                )
                rights.append(factor(jnp.concatenate([place] * 8, axis=0)))
            total = total + lax.dot_general(
                jnp.concatenate(lefts, axis=1),
                jnp.concatenate(rights, axis=1),
                contract,
                preferred_element_type=jnp.float32,
            )
        for c in range(chunks):
            out = (
                acc[pl.ds(c * TERM, TERM), :]
                + total[16 * c : 16 * c + 8]
                + total[16 * c + 8 : 16 * c + 16]
            )
            res[:, pl.ds(c * LANES, LANES)] = out[0:6]
            hess[pl.ds(c, 1), :] = out[6:7]

        stores = [
            pltpu.make_async_copy(res, res_hbm, out_sem.at[0]),
            pltpu.make_async_copy(hess, hess_hbm, out_sem.at[1]),
        ]
        for store in stores:
            store.start()

        @pl.loop(0, LISTS)
        def _(k):
            @pl.when(inside(me + list_offset(k)))
            def _():
                push(k).wait_send()

            @pl.when(inside(me - list_offset(k)))
            def _():
                push_back(k).wait_send()

        for store in stores:
            store.wait()

    return kernel


def shards(
    ndev,
    stress,
    stress_dir,
    adjoint,
    relax,
    relax_dir,
    connect,
    mass_mat,
    adv_mat,
    vel_grad,
    send_list,
    elem_count,
):
    nodes = stress.shape[1]
    elems = connect.shape[1]
    chunks = nodes // LANES
    steps = elems // ELEM_BLOCK // 2
    f32, i32 = jnp.float32, jnp.int32

    def by_groups(matrix, rows):
        split = matrix.reshape(-1, rows, elems // LANES, LANES)
        return split.transpose(0, 2, 1, 3).reshape(-1, LANES)

    args = (
        stress,
        stress_dir,
        adjoint,
        relax.reshape(chunks, LANES),
        relax_dir.reshape(chunks, LANES),
        by_groups(connect, 4),
        by_groups(mass_mat, 8),
        by_groups(adv_mat, 8),
        vel_grad,
        send_list.reshape(LISTS, LANES),
        elem_count,
    )
    hbm = pl.BlockSpec(memory_space=pl.ANY)
    res, hess = pl.pallas_call(
        make_kernel(ndev, nodes, elems),
        out_shape=(
            jax.ShapeDtypeStruct((6, nodes), f32),
            jax.ShapeDtypeStruct((chunks, LANES), f32),
        ),
        in_specs=[hbm] * 10 + [pl.BlockSpec(memory_space=pltpu.SMEM)],
        out_specs=(hbm, hbm),
        scratch_shapes=[
            pltpu.VMEM((6, nodes), f32),
            pltpu.VMEM((6, nodes), f32),
            pltpu.VMEM((6, nodes), f32),
            pltpu.VMEM((chunks, LANES), f32),
            pltpu.VMEM((chunks, LANES), f32),
            pltpu.VMEM((elems // 32, LANES), i32),
            pltpu.VMEM((elems // 8, LANES), f32),
            pltpu.VMEM((elems // 8, LANES), f32),
            pltpu.VMEM((9, elems), f32),
            pltpu.VMEM((LISTS, LANES), i32),
            pltpu.VMEM((6, nodes), f32),
            pltpu.VMEM((chunks, LANES), f32),
            pltpu.VMEM(((chunks + 1) * ROWS, LANES), f32),
            pltpu.VMEM((LISTS, ROWS, LANES), f32),
            pltpu.VMEM((LISTS, ROWS, LANES), f32),
            pltpu.VMEM((2, WIN * ROWS, LANES), f32),
            pltpu.VMEM((steps, 80, 8, LANES), f32),
            pltpu.VMEM((elems // 16, LANES), f32),
            pltpu.VMEM((elems // LANES, LANES), f32),
            pltpu.VMEM((2, 32, LANES), f32),
            pltpu.VMEM((4, 8 * TERM, LANES), f32),
            pltpu.VMEM(((chunks + 1) * TERM, LANES), f32),
            pltpu.VMEM((LISTS, TERM, LANES), f32),
            pltpu.VMEM((LISTS, TERM, LANES), f32),
            pltpu.SemaphoreType.DMA((10,)),
            pltpu.SemaphoreType.DMA((2,)),
            pltpu.SemaphoreType.DMA((LISTS,)),
            pltpu.SemaphoreType.DMA((LISTS,)),
            pltpu.SemaphoreType.DMA((LISTS,)),
            pltpu.SemaphoreType.DMA((LISTS,)),
        ],
        compiler_params=pltpu.CompilerParams(
            collective_id=0,
            has_side_effects=True,
            vmem_limit_bytes=48 * 1024 * 1024,
        ),
    )(*args)
    return res, hess.reshape(nodes)


def solution(mesh):
    ndev = mesh.shape["dom"]

    def run(*args):
        return shards(ndev, *args)

    return jax.shard_map(
        run,
        mesh=mesh,
        in_specs=(
            P(None, "dom"),
            P(None, "dom"),
            P(None, "dom"),
            P("dom"),
            P("dom"),
            P(None, "dom"),
            P(None, "dom"),
            P(None, "dom"),
            P(None, "dom"),
            P("dom"),
            P("dom"),
        ),
        out_specs=(P(None, "dom"), P("dom")),
        check_vma=False,
    )
```

```python
import jax
import jax.numpy as jnp
from jax import lax
from jax.experimental import pallas as pl
from jax.experimental.pallas import tpu as pltpu
from jax.sharding import PartitionSpec as P

HOPS = 8
LISTS = 2 * HOPS
ELEM_BLOCK = 512
KAPPA = 0.5
PAIRS = ((0, 0), (1, 1), (2, 2), (0, 1), (0, 2), (1, 2))
LAYOUT = ((0, 3, 4), (3, 1, 5), (4, 5, 2))

LANES = 128
ROWS = 24
TAU, LAM, DLAM, DIR, ADJ = 0, 6, 7, 8, 16
FIELD_ROWS = tuple(range(0, 14)) + tuple(range(16, 22))
WIN = 3
TERM = 8

GATHER = lax.GatherDimensionNumbers(
    offset_dims=(),
    collapsed_slice_dims=(1,),
    start_index_map=(1,),
    operand_batching_dims=(0,),
    start_indices_batching_dims=(0,),
)


def pick_lanes(table, lane):
    return lax.gather(
        table,
        lane[:, :, None],
        GATHER,
        slice_sizes=(1, 1),
        mode=lax.GatherScatterMode.PROMISE_IN_BOUNDS,
    )


def list_offset(index):
    return jnp.where(index < HOPS, index + 1, HOPS - 1 - index)


def row_of(ref, row, height=8):
    return jnp.broadcast_to(ref[pl.ds(row, 1), :], (height, LANES))


def two_parts(values):
    high = values.astype(jnp.bfloat16)
    low = (values - high.astype(jnp.float32)).astype(jnp.bfloat16)
    return jnp.concatenate([high, low], axis=0)


def symmetric_product(left, right):
    prod = [
        [
            left[row][0] * right[LAYOUT[0][col]]
            + left[row][1] * right[LAYOUT[1][col]]
            + left[row][2] * right[LAYOUT[2][col]]
            for col in range(3)
        ]
        for row in range(3)
    ]
    return [prod[row][col] + prod[col][row] for row, col in PAIRS]


def make_kernel(ndev, nodes, elems):
    chunks = nodes // LANES
    nblocks = elems // ELEM_BLOCK
    groups = ELEM_BLOCK // LANES
    steps = nblocks // 2
    span = max(nblocks - 1, 1)
    window = WIN * LANES

    def kernel(
        stress_hbm,
        dir_hbm,
        adj_hbm,
        relax_hbm,
        rdir_hbm,
        conn_hbm,
        mass_hbm,
        adv_hbm,
        grad_hbm,
        send_hbm,
        count_ref,
        res_hbm,
        hess_hbm,
        stress,
        sdir,
        adjoint,
        relax,
        rdir,
        conn,
        mass,
        adv,
        grad,
        send,
        res,
        hess,
        fields,
        payload,
        ghosts,
        rolled0,
        rolled1,
        table0,
        table1,
        values,
        gradv,
        grad8,
        gtable0,
        gtable1,
        merged0,
        merged1,
        index0,
        index1,
        terms0,
        terms1,
        acc,
        gout,
        returned,
        in_sem,
        out_sem,
        send_sem,
        recv_sem,
        back_sem,
        ret_sem,
    ):
        me = lax.axis_index("dom")
        loads = [
            pltpu.make_async_copy(src, dst, in_sem.at[i])
            for i, (src, dst) in enumerate(
                [
                    (stress_hbm, stress),
                    (dir_hbm, sdir),
                    (adj_hbm, adjoint),
                    (relax_hbm, relax),
                    (rdir_hbm, rdir),
                    (send_hbm, send),
                    (conn_hbm, conn),
                    (grad_hbm, grad),
                    (mass_hbm, mass),
                    (adv_hbm, adv),
                ]
            )
        ]
        for load in loads:
            load.start()

        def inside(device):
            return (device >= 0) & (device < ndev)

        barrier = pltpu.get_barrier_semaphore()

        @pl.loop(0, LISTS)
        def _(k):
            target = me + list_offset(k)

            @pl.when(inside(target))
            def _():
                pl.semaphore_signal(
                    barrier, inc=1, device_id=(target,), device_id_type=pl.DeviceIdType.MESH
                )

        zeros = jnp.zeros((8, LANES), jnp.float32)
        lane = lax.broadcasted_iota(jnp.int32, (8, LANES), 1)
        sub = lax.broadcasted_iota(jnp.int32, (8, LANES), 0)
        upper = sub >= groups

        for load in loads[:6]:
            load.wait()

        for c in range(chunks):
            cut = pl.ds(c * LANES, LANES)
            for base in (TAU, DIR, ADJ):
                fields[pl.ds(c * ROWS + base, 8), :] = zeros
            fields[pl.ds(c * ROWS + TAU, 6), :] = stress[:, cut]
            fields[pl.ds(c * ROWS + LAM, 1), :] = relax[pl.ds(c, 1), :]
            fields[pl.ds(c * ROWS + DLAM, 1), :] = rdir[pl.ds(c, 1), :]
            fields[pl.ds(c * ROWS + DIR, 6), :] = sdir[:, cut]
            fields[pl.ds(c * ROWS + ADJ, 6), :] = adjoint[:, cut]
        for base in (TAU, DIR, ADJ):
            fields[pl.ds(chunks * ROWS + base, 8), :] = zeros

        @pl.loop(0, LISTS)
        def _(k):
            entry = row_of(send, k)
            place = entry & (LANES - 1)
            chunk = entry >> 7
            picked = [zeros, zeros, zeros]
            for c in range(chunks):
                here = chunk == c
                for t in range(3):
                    got = pick_lanes(fields[pl.ds(c * ROWS + 8 * t, 8), :], place)
                    picked[t] = jnp.where(here, got, picked[t])
            for t in range(3):
                payload[k, pl.ds(8 * t, 8), :] = picked[t]

        first_up = jnp.minimum(HOPS, ndev - 1 - me)
        first_down = jnp.minimum(HOPS, me)
        pl.semaphore_wait(barrier, first_up + first_down)

        def push(k):
            target = me + list_offset(k)
            return pltpu.make_async_remote_copy(
                src_ref=payload.at[k],
                dst_ref=ghosts.at[k],
                send_sem=send_sem.at[k],
                recv_sem=recv_sem.at[k],
                device_id=(target,),
                device_id_type=pl.DeviceIdType.MESH,
            )

        def push_back(k):
            target = me - list_offset(k)
            return pltpu.make_async_remote_copy(
                src_ref=gout.at[k],
                dst_ref=returned.at[k],
                send_sem=back_sem.at[k],
                recv_sem=ret_sem.at[k],
                device_id=(target,),
                device_id_type=pl.DeviceIdType.MESH,
            )

        @pl.loop(0, LISTS)
        def _(k):
            @pl.when(inside(me + list_offset(k)))
            def _():
                push(k).start()

        for i in range(chunks + 1):
            acc[pl.ds(i * TERM, TERM), :] = zeros
        for i in range(LISTS):
            gout[i] = zeros
        for terms in (terms0, terms1):
            for k in range(4):
                for g in range(8):
                    terms[k, pl.ds(g * TERM, TERM), :] = zeros
        for k in range(4):
            index1[0, pl.ds(8 * k, 8), :] = zeros
            index1[1, pl.ds(8 * k, 8), :] = zeros - 1.0

        for load in loads[6:8]:
            load.wait()

        def starts_of(pair):
            one = (2 * pair) * (nodes - window) // span
            two = (2 * pair + 1) * (nodes - window) // span
            return one, two

        def relative(pair, k):
            one, two = starts_of(pair)
            lists_one = (2 * pair) % LISTS
            node = conn[pl.ds(pair * 32 + k, 8, stride=4), :]
            start = jnp.where(upper, two, one)
            ghost0 = nodes + LANES * jnp.where(upper, lists_one + 1, lists_one) - window
            return node - jnp.where(node >= nodes, ghost0, start)

        def prepare(pair, rolled, table):
            for which, start in enumerate(starts_of(pair)):
                chunk0 = start // LANES
                shift = start % LANES
                keep = lane < LANES - shift
                for t in range(3):
                    turned = [
                        pltpu.roll(
                            fields[
                                pl.ds(pl.multiple_of((chunk0 + i) * ROWS + 8 * t, 8), 8), :
                            ],
                            (LANES - shift) % LANES,
                            1,
                        )
                        for i in range(WIN + 1)
                    ]
                    for i in range(WIN):
                        rolled[which, pl.ds(i * ROWS + 8 * t, 8), :] = jnp.where(
                            keep, turned[i], turned[i + 1]
                        )
            for n, row in enumerate(FIELD_ROWS):
                for i in range(WIN):
                    table[n * WIN + i] = jnp.where(
                        upper,
                        row_of(rolled.at[1], i * ROWS + row),
                        row_of(rolled.at[0], i * ROWS + row),
                    )

        def gather_owned(pair, table):
            for k in range(4):
                rel = relative(pair, k)
                place = rel & (LANES - 1)
                first = rel < LANES
                second = rel < 2 * LANES
                for n in range(20):
                    a, b, c = [pick_lanes(table[n * WIN + i], place) for i in range(WIN)]
                    values[pair, k * 20 + n] = jnp.where(first, a, jnp.where(second, b, c))
            for j in range(8):
                cut = pl.ds(pl.multiple_of((pair * 8 + j) * LANES, LANES), LANES)
                gradv[pl.ds(pl.multiple_of((pair * 8 + j) * 8, 8), 8), :] = grad[0:8, cut]
                grad8[pl.ds(pair * 8 + j, 1), :] = grad[8:9, cut]

        prepare(0, rolled0, table0)

        @pl.loop(0, steps // 2)
        def _(i):
            gather_owned(2 * i, table0)
            prepare(2 * i + 1, rolled1, table1)
            gather_owned(2 * i + 1, table1)
            prepare(jnp.minimum(2 * i + 2, steps - 1), rolled0, table0)

        for load in loads[8:]:
            load.wait()

        count = count_ref[0]
        columns = lax.broadcasted_iota(jnp.int32, (LANES, LANES), 0).astype(jnp.bfloat16)
        one16 = jnp.ones((LANES, LANES), jnp.bfloat16)
        zero16 = jnp.zeros((LANES, LANES), jnp.bfloat16)
        contract = (((1,), (1,)), ((), ()))

        def factor(place_row):
            return jnp.where(columns == place_row, one16, zero16)

        def gather_ghosts(pair, gtable, merged):
            listed = (2 * pair) % LISTS
            for n, row in enumerate(FIELD_ROWS):
                gtable[n] = jnp.where(
                    upper, row_of(ghosts.at[listed + 1], row), row_of(ghosts.at[listed], row)
                )
            for k in range(4):
                rel = relative(pair, k)
                place = rel & (LANES - 1)
                ghostly = rel >= window
                for n in range(20):
                    merged[k * 20 + n] = jnp.where(
                        ghostly, pick_lanes(gtable[n], place), values[pair, k * 20 + n]
                    )

        def algebra(pair, merged, terms, index_rows):
            got = [[merged[k * 20 + n] for n in range(20)] for k in range(4)]
            lam_e = 0.25 * (got[0][6] + got[1][6] + got[2][6] + got[3][6])
            dlam_e = 0.25 * (got[0][7] + got[1][7] + got[2][7] + got[3][7])
            vel = [
                gradv[pl.ds(pair * 64 + i, 8, stride=8), :] for i in range(8)
            ] + [grad8[pl.ds(pl.multiple_of(pair * 8, 8), 8), :]]
            tdir, gin, wsum, usum = [], [], [], []
            for k in range(4):
                tau = got[k][0:6]
                t = got[k][8:14]
                half = [KAPPA * s for s in tau]
                quarter = [0.5 * s for s in half]
                left_g = [
                    [half[LAYOUT[r][c]] - vel[3 * r + c] for c in range(3)] for r in range(3)
                ]
                left_b = [
                    [quarter[LAYOUT[r][c]] - vel[3 * r + c] for c in range(3)] for r in range(3)
                ]
                b_in = symmetric_product(left_b, tau)
                tdir.append(t)
                gin.append(symmetric_product(left_g, t))
                wsum.append([dlam_e * s for s in tau])
                usum.append([t[c] + dlam_e * b_in[c] for c in range(6)])
            score = zeros
            for a in range(4):
                mat, adm = [], []
                for b in range(4):
                    entry = 4 * a + b
                    at = (entry // 8) * (elems // 16) + pair * 64 + entry % 8
                    mat.append(mass[pl.ds(at, 8, stride=8), :])
                    adm.append(adv[pl.ds(at, 8, stride=8), :])
                for c in range(6):
                    g = adm[0] * tdir[0][c] + mat[0] * gin[0][c]
                    d = adm[0] * wsum[0][c] + mat[0] * usum[0][c]
                    for b in range(1, 4):
                        g = g + (adm[b] * tdir[b][c] + mat[b] * gin[b][c])
                        d = d + (adm[b] * wsum[b][c] + mat[b] * usum[b][c])
                    score = score + got[a][14 + c] * g
                    terms[a, pl.ds(c, 8, stride=TERM), :] = d + lam_e * g
            score = 0.25 * score
            for a in range(4):
                terms[a, pl.ds(6, 8, stride=TERM), :] = score
            live = (pair * 8 + sub) * LANES + lane < count
            for k in range(4):
                rel = relative(pair, k)
                index_rows[0, pl.ds(8 * k, 8), :] = (rel & (LANES - 1)).astype(jnp.float32)
                index_rows[1, pl.ds(8 * k, 8), :] = jnp.where(live, rel >> 7, -1).astype(
                    jnp.float32
                )

        def scatter(pair, terms, index_rows):
            listed = (2 * pair) % LISTS
            for which, start in enumerate(starts_of(pair)):
                lefts, rights = [], []
                for k in range(4):
                    for j in range(groups):
                        g = which * groups + j
                        part = two_parts(terms[k, pl.ds(g * TERM, TERM), :])
                        chunk = row_of(index_rows.at[1], 8 * k + g, 16).astype(jnp.bfloat16)
                        place = row_of(index_rows.at[0], 8 * k + g, 16).astype(jnp.bfloat16)
                        lefts.append(
                            jnp.concatenate(
                                [
                                    jnp.where(chunk == float(i), part, zero16[:16])
                                    for i in range(4)
                                ],
                                axis=0,
                            )
                        )
                        rights.append(factor(jnp.concatenate([place] * 8, axis=0)))
                total = lax.dot_general(
                    jnp.concatenate(lefts, axis=1),
                    jnp.concatenate(rights, axis=1),
                    contract,
                    preferred_element_type=jnp.float32,
                )
                sums = [
                    total[16 * i : 16 * i + 8] + total[16 * i + 8 : 16 * i + 16]
                    for i in range(4)
                ]
                chunk0 = start // LANES
                shift = start % LANES
                turned = [pltpu.roll(sums[i], shift, 1) for i in range(WIN)]
                later = lane >= shift
                for i in range(WIN + 1):
                    if i == 0:
                        add = jnp.where(later, turned[0], 0.0)
                    elif i == WIN:
                        add = jnp.where(later, 0.0, turned[WIN - 1])
                    else:
                        add = jnp.where(later, turned[i], turned[i - 1])
                    at = pl.ds(pl.multiple_of((chunk0 + i) * TERM, TERM), TERM)
                    acc[at, :] = acc[at, :] + add
                gout[listed + which] = gout[listed + which] + sums[WIN]

        turns = LISTS // 2

        @pl.loop(0, LISTS)
        def _(k):
            @pl.when(inside(me - list_offset(k)))
            def _():
                push(k).wait_recv()

        def give_back(turn):
            for which in range(2):
                k = 2 * turn + which

                @pl.when(inside(me - list_offset(k)) & (k >= 0))
                def _():
                    push_back(k).start()

        gather_ghosts(0, gtable0, merged0)
        gather_ghosts(turns, gtable1, merged1)

        @pl.loop(0, turns)
        def _(turn):
            later = jnp.minimum(turn + 1, turns - 1)
            before = jnp.maximum(turn - 1, 0)
            algebra(turn, merged0, terms0, index0)
            scatter(before + turns, terms1, index1)
            gather_ghosts(later, gtable0, merged0)
            algebra(turn + turns, merged1, terms1, index1)
            scatter(turn, terms0, index0)
            gather_ghosts(later + turns, gtable1, merged1)
            give_back(turn - 1)

        scatter(2 * turns - 1, terms1, index1)
        give_back(turns - 1)

        @pl.loop(0, LISTS)
        def _(k):
            @pl.when(inside(me + list_offset(k)))
            def _():
                push_back(k).wait_recv()

        total = jnp.zeros((chunks * 2 * TERM, LANES), jnp.float32)
        for pairing in range(LISTS // 2):
            lefts, rights = [], []
            for k in (2 * pairing, 2 * pairing + 1):
                entry = row_of(send, k)
                part = two_parts(jnp.where(entry >= 0, returned[k], 0.0))
                entry16 = row_of(send, k, 16)
                chunk = (entry16 >> 7).astype(jnp.float32).astype(jnp.bfloat16)
                place = (entry16 & (LANES - 1)).astype(jnp.float32).astype(jnp.bfloat16)
                lefts.append(
                    jnp.concatenate(
                        [
                            jnp.where(chunk == float(i), part, zero16[:16])
                            for i in range(chunks)
                        ],
                        axis=0,
                    )
                )
                rights.append(factor(jnp.concatenate([place] * 8, axis=0)))
            total = total + lax.dot_general(
                jnp.concatenate(lefts, axis=1),
                jnp.concatenate(rights, axis=1),
                contract,
                preferred_element_type=jnp.float32,
            )
        for c in range(chunks):
            out = (
                acc[pl.ds(c * TERM, TERM), :]
                + total[16 * c : 16 * c + 8]
                + total[16 * c + 8 : 16 * c + 16]
            )
            res[:, pl.ds(c * LANES, LANES)] = out[0:6]
            hess[pl.ds(c, 1), :] = out[6:7]

        stores = [
            pltpu.make_async_copy(res, res_hbm, out_sem.at[0]),
            pltpu.make_async_copy(hess, hess_hbm, out_sem.at[1]),
        ]
        for store in stores:
            store.start()

        @pl.loop(0, LISTS)
        def _(k):
            @pl.when(inside(me + list_offset(k)))
            def _():
                push(k).wait_send()

            @pl.when(inside(me - list_offset(k)))
            def _():
                push_back(k).wait_send()

        for store in stores:
            store.wait()

    return kernel


def shards(
    ndev,
    stress,
    stress_dir,
    adjoint,
    relax,
    relax_dir,
    connect,
    mass_mat,
    adv_mat,
    vel_grad,
    send_list,
    elem_count,
):
    nodes = stress.shape[1]
    elems = connect.shape[1]
    chunks = nodes // LANES
    steps = elems // ELEM_BLOCK // 2
    f32, i32 = jnp.float32, jnp.int32

    def by_groups(matrix, rows):
        split = matrix.reshape(-1, rows, elems // LANES, LANES)
        return split.transpose(0, 2, 1, 3).reshape(-1, LANES)

    args = (
        stress,
        stress_dir,
        adjoint,
        relax.reshape(chunks, LANES),
        relax_dir.reshape(chunks, LANES),
        by_groups(connect, 4),
        by_groups(mass_mat, 8),
        by_groups(adv_mat, 8),
        vel_grad,
        send_list.reshape(LISTS, LANES),
        elem_count,
    )
    hbm = pl.BlockSpec(memory_space=pl.ANY)
    res, hess = pl.pallas_call(
        make_kernel(ndev, nodes, elems),
        out_shape=(
            jax.ShapeDtypeStruct((6, nodes), f32),
            jax.ShapeDtypeStruct((chunks, LANES), f32),
        ),
        in_specs=[hbm] * 10 + [pl.BlockSpec(memory_space=pltpu.SMEM)],
        out_specs=(hbm, hbm),
        scratch_shapes=[
            pltpu.VMEM((6, nodes), f32),
            pltpu.VMEM((6, nodes), f32),
            pltpu.VMEM((6, nodes), f32),
            pltpu.VMEM((chunks, LANES), f32),
            pltpu.VMEM((chunks, LANES), f32),
            pltpu.VMEM((elems // 32, LANES), i32),
            pltpu.VMEM((elems // 8, LANES), f32),
            pltpu.VMEM((elems // 8, LANES), f32),
            pltpu.VMEM((9, elems), f32),
            pltpu.VMEM((LISTS, LANES), i32),
            pltpu.VMEM((6, nodes), f32),
            pltpu.VMEM((chunks, LANES), f32),
            pltpu.VMEM(((chunks + 1) * ROWS, LANES), f32),
            pltpu.VMEM((LISTS, ROWS, LANES), f32),
            pltpu.VMEM((LISTS, ROWS, LANES), f32),
            pltpu.VMEM((2, WIN * ROWS, LANES), f32),
            pltpu.VMEM((2, WIN * ROWS, LANES), f32),
            pltpu.VMEM((20 * WIN, 8, LANES), f32),
            pltpu.VMEM((20 * WIN, 8, LANES), f32),
            pltpu.VMEM((steps, 80, 8, LANES), f32),
            pltpu.VMEM((elems // 16, LANES), f32),
            pltpu.VMEM((elems // LANES, LANES), f32),
            pltpu.VMEM((20, 8, LANES), f32),
            pltpu.VMEM((20, 8, LANES), f32),
            pltpu.VMEM((80, 8, LANES), f32),
            pltpu.VMEM((80, 8, LANES), f32),
            pltpu.VMEM((2, 32, LANES), f32),
            pltpu.VMEM((2, 32, LANES), f32),
            pltpu.VMEM((4, 8 * TERM, LANES), f32),
            pltpu.VMEM((4, 8 * TERM, LANES), f32),
            pltpu.VMEM(((chunks + 1) * TERM, LANES), f32),
            pltpu.VMEM((LISTS, TERM, LANES), f32),
            pltpu.VMEM((LISTS, TERM, LANES), f32),
            pltpu.SemaphoreType.DMA((10,)),
            pltpu.SemaphoreType.DMA((2,)),
            pltpu.SemaphoreType.DMA((LISTS,)),
            pltpu.SemaphoreType.DMA((LISTS,)),
            pltpu.SemaphoreType.DMA((LISTS,)),
            pltpu.SemaphoreType.DMA((LISTS,)),
        ],
        compiler_params=pltpu.CompilerParams(
            collective_id=0,
            has_side_effects=True,
            vmem_limit_bytes=62 * 1024 * 1024,
        ),
    )(*args)
    return res, hess.reshape(nodes)


def solution(mesh):
    ndev = mesh.shape["dom"]

    def run(*args):
        return shards(ndev, *args)

    return jax.shard_map(
        run,
        mesh=mesh,
        in_specs=(
            P(None, "dom"),
            P(None, "dom"),
            P(None, "dom"),
            P("dom"),
            P("dom"),
            P(None, "dom"),
            P(None, "dom"),
            P(None, "dom"),
            P(None, "dom"),
            P("dom"),
            P("dom"),
        ),
        out_specs=(P(None, "dom"), P("dom")),
        check_vma=False,
    )
```

```python
import jax
import jax.numpy as jnp
from jax import lax
from jax.experimental import pallas as pl
from jax.experimental.pallas import tpu as pltpu
from jax.sharding import PartitionSpec as P

HOPS = 8
LISTS = 2 * HOPS
ELEM_BLOCK = 512
KAPPA = 0.5
PAIRS = ((0, 0), (1, 1), (2, 2), (0, 1), (0, 2), (1, 2))
LAYOUT = ((0, 3, 4), (3, 1, 5), (4, 5, 2))

LANES = 128
ROWS = 24
TAU, LAM, DLAM, DIR, ADJ = 0, 6, 7, 8, 16
FIELD_ROWS = tuple(range(0, 14)) + tuple(range(16, 22))
WIN = 3
TERM = 8

GATHER = lax.GatherDimensionNumbers(
    offset_dims=(),
    collapsed_slice_dims=(1,),
    start_index_map=(1,),
    operand_batching_dims=(0,),
    start_indices_batching_dims=(0,),
)


def pick_lanes(table, lane):
    return lax.gather(
        table,
        lane[:, :, None],
        GATHER,
        slice_sizes=(1, 1),
        mode=lax.GatherScatterMode.PROMISE_IN_BOUNDS,
    )


def list_offset(index):
    return jnp.where(index < HOPS, index + 1, HOPS - 1 - index)


def row_of(ref, row, height=8):
    return jnp.broadcast_to(ref[pl.ds(row, 1), :], (height, LANES))


def two_parts(values):
    high = values.astype(jnp.bfloat16).astype(jnp.float32)
    return jnp.concatenate([high, values - high], axis=0).astype(jnp.bfloat16)


def symmetric_product(left, right):
    prod = [
        [
            left[row][0] * right[LAYOUT[0][col]]
            + left[row][1] * right[LAYOUT[1][col]]
            + left[row][2] * right[LAYOUT[2][col]]
            for col in range(3)
        ]
        for row in range(3)
    ]
    return [prod[row][col] + prod[col][row] for row, col in PAIRS]


def make_kernel(ndev, nodes, elems):
    chunks = nodes // LANES
    nblocks = elems // ELEM_BLOCK
    groups = ELEM_BLOCK // LANES
    span = max(nblocks - 1, 1)
    window = WIN * LANES
    turns = LISTS // 2

    def kernel(
        stress_hbm,
        dir_hbm,
        adj_hbm,
        relax_hbm,
        rdir_hbm,
        conn_hbm,
        mass_hbm,
        adv_hbm,
        grad_hbm,
        send_hbm,
        count_ref,
        res_hbm,
        hess_hbm,
        stress,
        sdir,
        adjoint,
        relax,
        rdir,
        conn,
        mass,
        adv,
        grad,
        send,
        res,
        hess,
        fields,
        payload,
        ghosts,
        rolled0,
        rolled1,
        table0,
        table1,
        owned0,
        owned1,
        vel0,
        vel1,
        vel80,
        vel81,
        mvel0,
        mvel1,
        mvel80,
        mvel81,
        gtable0,
        gtable1,
        merged0,
        merged1,
        index,
        rels,
        terms0,
        terms1,
        parts0,
        parts1,
        acc,
        gout,
        returned,
        in_sem,
        out_sem,
        send_sem,
        recv_sem,
        back_sem,
        ret_sem,
    ):
        me = lax.axis_index("dom")
        loads = [
            pltpu.make_async_copy(src, dst, in_sem.at[i])
            for i, (src, dst) in enumerate(
                [
                    (stress_hbm, stress),
                    (dir_hbm, sdir),
                    (adj_hbm, adjoint),
                    (relax_hbm, relax),
                    (rdir_hbm, rdir),
                    (send_hbm, send),
                    (conn_hbm, conn),
                    (grad_hbm, grad),
                    (mass_hbm, mass),
                    (adv_hbm, adv),
                ]
            )
        ]
        for load in loads:
            load.start()

        def inside(device):
            return (device >= 0) & (device < ndev)

        barrier = pltpu.get_barrier_semaphore()

        @pl.loop(0, LISTS)
        def _(k):
            target = me + list_offset(k)

            @pl.when(inside(target))
            def _():
                pl.semaphore_signal(
                    barrier, inc=1, device_id=(target,), device_id_type=pl.DeviceIdType.MESH
                )

        zeros = jnp.zeros((8, LANES), jnp.float32)
        lane = lax.broadcasted_iota(jnp.int32, (8, LANES), 1)
        sub = lax.broadcasted_iota(jnp.int32, (8, LANES), 0)
        upper = sub >= groups

        for load in loads[:6]:
            load.wait()

        for c in range(chunks):
            cut = pl.ds(c * LANES, LANES)
            for base in (TAU, DIR, ADJ):
                fields[pl.ds(c * ROWS + base, 8), :] = zeros
            fields[pl.ds(c * ROWS + TAU, 6), :] = 0.5 * KAPPA * stress[:, cut]
            fields[pl.ds(c * ROWS + LAM, 1), :] = relax[pl.ds(c, 1), :]
            fields[pl.ds(c * ROWS + DLAM, 1), :] = rdir[pl.ds(c, 1), :]
            fields[pl.ds(c * ROWS + DIR, 6), :] = sdir[:, cut]
            fields[pl.ds(c * ROWS + ADJ, 6), :] = adjoint[:, cut]
        for base in (TAU, DIR, ADJ):
            fields[pl.ds(chunks * ROWS + base, 8), :] = zeros

        def starts_of(pair):
            one = (2 * pair) * (nodes - window) // span
            two = (2 * pair + 1) * (nodes - window) // span
            return one, two

        def relative(pair, k):
            one, two = starts_of(pair)
            lists_one = (2 * pair) % LISTS
            node = conn[pl.ds(pair * 32 + k, 8, stride=4), :]
            start = jnp.where(upper, two, one)
            ghost0 = nodes + LANES * jnp.where(upper, lists_one + 1, lists_one) - window
            return node - jnp.where(node >= nodes, ghost0, start)

        count = count_ref[0]
        columns = lax.broadcasted_iota(jnp.int32, (LANES, LANES), 0).astype(jnp.bfloat16)
        one16 = jnp.ones((LANES, LANES), jnp.bfloat16)
        zero16 = jnp.zeros((LANES, LANES), jnp.bfloat16)
        contract = (((1,), (1,)), ((), ()))

        def factor(place_row):
            return jnp.where(columns == place_row, one16, zero16)

        def mark(pair):
            live = (pair * 8 + sub) * LANES + lane < count
            for k in range(4):
                rel = relative(pair, k)
                rels[pair, k] = rel
                index[pair, 0, pl.ds(8 * k, 8), :] = (rel & (LANES - 1)).astype(jnp.float32)
                index[pair, 1, pl.ds(8 * k, 8), :] = jnp.where(live, rel >> 7, -1).astype(
                    jnp.float32
                )

        for load in loads[6:7]:
            load.wait()

        @pl.loop(0, LISTS)
        def _(k):
            entry = row_of(send, k)
            place = entry & (LANES - 1)
            chunk = entry >> 7
            picked = [zeros, zeros, zeros]
            for c in range(chunks):
                here = chunk == c
                for t in range(3):
                    got = pick_lanes(fields[pl.ds(c * ROWS + 8 * t, 8), :], place)
                    picked[t] = jnp.where(here, got, picked[t])
            for t in range(3):
                payload[k, pl.ds(8 * t, 8), :] = picked[t]
            mark(k)

        first_up = jnp.minimum(HOPS, ndev - 1 - me)
        first_down = jnp.minimum(HOPS, me)
        pl.semaphore_wait(barrier, first_up + first_down)

        def push(k):
            target = me + list_offset(k)
            return pltpu.make_async_remote_copy(
                src_ref=payload.at[k],
                dst_ref=ghosts.at[k],
                send_sem=send_sem.at[k],
                recv_sem=recv_sem.at[k],
                device_id=(target,),
                device_id_type=pl.DeviceIdType.MESH,
            )

        def push_back(k):
            target = me - list_offset(k)
            return pltpu.make_async_remote_copy(
                src_ref=gout.at[k],
                dst_ref=returned.at[k],
                send_sem=back_sem.at[k],
                recv_sem=ret_sem.at[k],
                device_id=(target,),
                device_id_type=pl.DeviceIdType.MESH,
            )

        @pl.loop(0, LISTS)
        def _(k):
            @pl.when(inside(me + list_offset(k)))
            def _():
                push(k).start()

        for i in range(chunks + 1):
            acc[pl.ds(i * TERM, TERM), :] = zeros
        for i in range(LISTS):
            gout[i] = zeros
        for i in range(2 * WIN):
            parts0[i] = zeros
        for terms in (terms0, terms1):
            for k in range(4):
                for g in range(8):
                    terms[k, pl.ds(g * TERM, TERM), :] = zeros
        loads[7].wait()

        def weave(one, two):
            spent = [0, 0]
            parts = [one, two]
            while parts[0] is not None or parts[1] is not None:
                which = 0 if spent[0] <= spent[1] else 1
                if parts[which] is None:
                    which = 1 - which
                cost = next(parts[which], None)
                if cost is None:
                    parts[which] = None
                else:
                    spent[which] += cost

        def run(*parts):
            for part in parts:
                for _ in part:
                    pass

        def prepare(pair, rolled, table):
            for which, start in enumerate(starts_of(pair)):
                chunk0 = start // LANES
                shift = start % LANES
                keep = lane < LANES - shift
                for t in range(3):
                    turned = [
                        pltpu.roll(
                            fields[
                                pl.ds(pl.multiple_of((chunk0 + i) * ROWS + 8 * t, 8), 8), :
                            ],
                            (LANES - shift) % LANES,
                            1,
                        )
                        for i in range(WIN + 1)
                    ]
                    for i in range(WIN):
                        rolled[which, pl.ds(i * ROWS + 8 * t, 8), :] = jnp.where(
                            keep, turned[i], turned[i + 1]
                        )
            yield 50
            for n, row in enumerate(FIELD_ROWS):
                for i in range(WIN):
                    table[n * WIN + i] = jnp.where(
                        upper,
                        row_of(rolled.at[1], i * ROWS + row),
                        row_of(rolled.at[0], i * ROWS + row),
                    )
            yield 20

        def gather_owned(pair, table, owned, vel, vel8):
            for k in range(4):
                rel = rels[pair, k]
                place = rel & (LANES - 1)
                first = rel < LANES
                second = rel < 2 * LANES
                for n in range(20):
                    a, b, c = [pick_lanes(table[n * WIN + i], place) for i in range(WIN)]
                    owned[k * 20 + n] = jnp.where(first, a, jnp.where(second, b, c))
                    if n % 4 == 3:
                        yield 24
            for j in range(8):
                cut = pl.ds(pl.multiple_of((pair * 8 + j) * LANES, LANES), LANES)
                vel[pl.ds(j * 8, 8), :] = grad[0:8, cut]
                vel8[pl.ds(j, 1), :] = grad[8:9, cut]
            yield 8

        run(prepare(0, rolled0, table0), prepare(turns, rolled1, table1))
        run(gather_owned(0, table0, owned0, vel0, vel80), prepare(1, rolled0, table0))
        run(gather_owned(turns, table1, owned1, vel1, vel81), prepare(turns + 1, rolled1, table1))

        for load in loads[8:]:
            load.wait()

        def gather_ghosts(pair, gtable, owned, vel_in, vel8_in, merged, vel, vel8):
            listed = (2 * pair) % LISTS
            for n, row in enumerate(FIELD_ROWS):
                gtable[n] = jnp.where(
                    upper, row_of(ghosts.at[listed + 1], row), row_of(ghosts.at[listed], row)
                )
            vel[...] = vel_in[...]
            vel8[...] = vel8_in[...]
            yield 15
            for k in range(4):
                rel = rels[pair, k]
                place = rel & (LANES - 1)
                ghostly = rel >= window
                for n in range(20):
                    merged[k * 20 + n] = jnp.where(
                        ghostly, pick_lanes(gtable[n], place), owned[k * 20 + n]
                    )
                    if n % 10 == 9:
                        yield 20

        def algebra(pair, merged, vel_rows, vel8, terms):
            def got(k, n):
                return merged[k * 20 + n]

            lam_e = 0.25 * (got(0, 6) + got(1, 6) + got(2, 6) + got(3, 6))
            dlam4 = got(0, 7) + got(1, 7) + got(2, 7) + got(3, 7)
            vel = [vel_rows[pl.ds(i, 8, stride=8), :] for i in range(8)] + [vel8[...]]
            tdir, gin, wsum, usum = [], [], [], []
            for k in range(4):
                tau = [got(k, c) for c in range(6)]
                t = [got(k, 8 + c) for c in range(6)]
                left_b = [
                    [tau[LAYOUT[r][c]] - vel[3 * r + c] for c in range(3)] for r in range(3)
                ]
                left_g = [
                    [left_b[r][c] + tau[LAYOUT[r][c]] for c in range(3)] for r in range(3)
                ]
                b_in = symmetric_product(left_b, tau)
                tdir.append(t)
                gin.append(symmetric_product(left_g, t))
                wsum.append([dlam4 * s for s in tau])
                usum.append([t[c] + dlam4 * b_in[c] for c in range(6)])
                yield 38
            score = zeros
            for a in range(4):
                mat, adm = [], []
                for b in range(4):
                    entry = 4 * a + b
                    at = (entry // 8) * (elems // 16) + pair * 64 + entry % 8
                    mat.append(mass[pl.ds(at, 8, stride=8), :])
                    adm.append(adv[pl.ds(at, 8, stride=8), :])
                for c in range(6):
                    g = adm[0] * tdir[0][c] + mat[0] * gin[0][c]
                    d = adm[0] * wsum[0][c] + mat[0] * usum[0][c]
                    for b in range(1, 4):
                        g = g + (adm[b] * tdir[b][c] + mat[b] * gin[b][c])
                        d = d + (adm[b] * wsum[b][c] + mat[b] * usum[b][c])
                    score = score + got(a, 14 + c) * g
                    terms[a, pl.ds(c, 8, stride=TERM), :] = d + lam_e * g
                    if c % 2 == 1:
                        yield 17
            score = 0.25 * score
            for a in range(4):
                terms[a, pl.ds(6, 8, stride=TERM), :] = score
            yield 2

        def scatter(pair, terms, parts):
            listed = (2 * pair) % LISTS
            for which in range(2):
                lefts, rights = [], []
                for k in range(4):
                    for j in range(groups):
                        g = which * groups + j
                        part = two_parts(terms[k, pl.ds(g * TERM, TERM), :])
                        chunk = row_of(index.at[pair, 1], 8 * k + g, 16).astype(jnp.bfloat16)
                        place = row_of(index.at[pair, 0], 8 * k + g, 16).astype(jnp.bfloat16)
                        rights.append(factor(jnp.concatenate([place] * 8, axis=0)))
                        lefts.append(
                            jnp.concatenate(
                                [
                                    jnp.where(chunk == float(i), part, zero16[:16])
                                    for i in range(4)
                                ],
                                axis=0,
                            )
                        )
                    yield 32
                total = lax.dot_general(
                    jnp.concatenate(lefts, axis=1),
                    jnp.concatenate(rights, axis=1),
                    contract,
                    preferred_element_type=jnp.float32,
                )
                sums = [
                    total[16 * i : 16 * i + 8] + total[16 * i + 8 : 16 * i + 16]
                    for i in range(4)
                ]
                for i in range(WIN):
                    parts[which * WIN + i] = sums[i]
                gout[listed + which] = gout[listed + which] + sums[WIN]
                yield 4

        def fold(pair, parts):
            for which, start in enumerate(starts_of(pair)):
                chunk0 = start // LANES
                shift = start % LANES
                turned = [pltpu.roll(parts[which * WIN + i], shift, 1) for i in range(WIN)]
                later = lane >= shift
                for i in range(WIN + 1):
                    if i == 0:
                        add = jnp.where(later, turned[0], 0.0)
                    elif i == WIN:
                        add = jnp.where(later, 0.0, turned[WIN - 1])
                    else:
                        add = jnp.where(later, turned[i], turned[i - 1])
                    at = pl.ds(pl.multiple_of((chunk0 + i) * TERM, TERM), TERM)
                    acc[at, :] = acc[at, :] + add
                yield 8

        def both(one, two):
            yield from one
            yield from two

        @pl.loop(0, LISTS)
        def _(k):
            @pl.when(inside(me - list_offset(k)))
            def _():
                push(k).wait_recv()

        def give_back(turn):
            for which in range(2):
                k = 2 * turn + which

                @pl.when(inside(me - list_offset(k)) & (k >= 0))
                def _():
                    push_back(k).start()

        def merge(turn, half):
            if half == 0:
                return gather_ghosts(
                    turn, gtable0, owned0, vel0, vel80, merged0, mvel0, mvel80
                )
            return gather_ghosts(
                turn + turns, gtable1, owned1, vel1, vel81, merged1, mvel1, mvel81
            )

        def look_ahead(turn, half):
            after = jnp.minimum(turn + 1, turns - 1)
            if half == 0:
                yield from gather_owned(turn, table0, owned0, vel0, vel80)
                yield from prepare(after, rolled0, table0)
            else:
                yield from gather_owned(turn + turns, table1, owned1, vel1, vel81)
                yield from prepare(after + turns, rolled1, table1)

        run(merge(0, 0), look_ahead(1, 0))

        @pl.loop(0, turns)
        def _(turn):
            before = jnp.maximum(turn - 1, 0)
            one = jnp.minimum(turn + 1, turns - 1)
            two = jnp.minimum(turn + 2, turns - 1)
            run(fold(before, parts0))
            weave(
                both(merge(turn, 1), look_ahead(one, 1)),
                both(
                    algebra(turn, merged0, mvel0, mvel80, terms0),
                    scatter(before + turns, terms1, parts1),
                ),
            )
            run(fold(before + turns, parts1))
            weave(
                both(merge(one, 0), look_ahead(two, 0)),
                both(
                    algebra(turn + turns, merged1, mvel1, mvel81, terms1),
                    scatter(turn, terms0, parts0),
                ),
            )
            give_back(turn - 1)

        run(
            scatter(2 * turns - 1, terms1, parts1),
            fold(turns - 1, parts0),
            fold(2 * turns - 1, parts1),
        )
        give_back(turns - 1)

        @pl.loop(0, LISTS)
        def _(k):
            @pl.when(inside(me + list_offset(k)))
            def _():
                push_back(k).wait_recv()

        total = jnp.zeros((chunks * 2 * TERM, LANES), jnp.float32)
        for pairing in range(LISTS // 2):
            lefts, rights = [], []
            for k in (2 * pairing, 2 * pairing + 1):
                entry = row_of(send, k)
                part = two_parts(jnp.where(entry >= 0, returned[k], 0.0))
                entry16 = row_of(send, k, 16)
                chunk = (entry16 >> 7).astype(jnp.float32).astype(jnp.bfloat16)
                place = (entry16 & (LANES - 1)).astype(jnp.float32).astype(jnp.bfloat16)
                lefts.append(
                    jnp.concatenate(
                        [
                            jnp.where(chunk == float(i), part, zero16[:16])
                            for i in range(chunks)
                        ],
                        axis=0,
                    )
                )
                rights.append(factor(jnp.concatenate([place] * 8, axis=0)))
            total = total + lax.dot_general(
                jnp.concatenate(lefts, axis=1),
                jnp.concatenate(rights, axis=1),
                contract,
                preferred_element_type=jnp.float32,
            )
        for c in range(chunks):
            out = (
                acc[pl.ds(c * TERM, TERM), :]
                + total[16 * c : 16 * c + 8]
                + total[16 * c + 8 : 16 * c + 16]
            )
            res[:, pl.ds(c * LANES, LANES)] = out[0:6]
            hess[pl.ds(c, 1), :] = out[6:7]

        stores = [
            pltpu.make_async_copy(res, res_hbm, out_sem.at[0]),
            pltpu.make_async_copy(hess, hess_hbm, out_sem.at[1]),
        ]
        for store in stores:
            store.start()

        @pl.loop(0, LISTS)
        def _(k):
            @pl.when(inside(me + list_offset(k)))
            def _():
                push(k).wait_send()

            @pl.when(inside(me - list_offset(k)))
            def _():
                push_back(k).wait_send()

        for store in stores:
            store.wait()

    return kernel


def shards(
    ndev,
    stress,
    stress_dir,
    adjoint,
    relax,
    relax_dir,
    connect,
    mass_mat,
    adv_mat,
    vel_grad,
    send_list,
    elem_count,
):
    nodes = stress.shape[1]
    elems = connect.shape[1]
    chunks = nodes // LANES
    f32, i32 = jnp.float32, jnp.int32

    def by_groups(matrix, rows):
        split = matrix.reshape(-1, rows, elems // LANES, LANES)
        return split.transpose(0, 2, 1, 3).reshape(-1, LANES)

    args = (
        stress,
        stress_dir,
        adjoint,
        relax.reshape(chunks, LANES),
        relax_dir.reshape(chunks, LANES),
        by_groups(connect, 4),
        by_groups(mass_mat, 8),
        by_groups(adv_mat, 8),
        vel_grad,
        send_list.reshape(LISTS, LANES),
        elem_count,
    )
    hbm = pl.BlockSpec(memory_space=pl.ANY)
    res, hess = pl.pallas_call(
        make_kernel(ndev, nodes, elems),
        out_shape=(
            jax.ShapeDtypeStruct((6, nodes), f32),
            jax.ShapeDtypeStruct((chunks, LANES), f32),
        ),
        in_specs=[hbm] * 10 + [pl.BlockSpec(memory_space=pltpu.SMEM)],
        out_specs=(hbm, hbm),
        scratch_shapes=[
            pltpu.VMEM((6, nodes), f32),
            pltpu.VMEM((6, nodes), f32),
            pltpu.VMEM((6, nodes), f32),
            pltpu.VMEM((chunks, LANES), f32),
            pltpu.VMEM((chunks, LANES), f32),
            pltpu.VMEM((elems // 32, LANES), i32),
            pltpu.VMEM((elems // 8, LANES), f32),
            pltpu.VMEM((elems // 8, LANES), f32),
            pltpu.VMEM((9, elems), f32),
            pltpu.VMEM((LISTS, LANES), i32),
            pltpu.VMEM((6, nodes), f32),
            pltpu.VMEM((chunks, LANES), f32),
            pltpu.VMEM(((chunks + 1) * ROWS, LANES), f32),
            pltpu.VMEM((LISTS, ROWS, LANES), f32),
            pltpu.VMEM((LISTS, ROWS, LANES), f32),
            pltpu.VMEM((2, WIN * ROWS, LANES), f32),
            pltpu.VMEM((2, WIN * ROWS, LANES), f32),
            pltpu.VMEM((20 * WIN, 8, LANES), f32),
            pltpu.VMEM((20 * WIN, 8, LANES), f32),
            pltpu.VMEM((80, 8, LANES), f32),
            pltpu.VMEM((80, 8, LANES), f32),
            pltpu.VMEM((64, LANES), f32),
            pltpu.VMEM((64, LANES), f32),
            pltpu.VMEM((8, LANES), f32),
            pltpu.VMEM((8, LANES), f32),
            pltpu.VMEM((64, LANES), f32),
            pltpu.VMEM((64, LANES), f32),
            pltpu.VMEM((8, LANES), f32),
            pltpu.VMEM((8, LANES), f32),
            pltpu.VMEM((20, 8, LANES), f32),
            pltpu.VMEM((20, 8, LANES), f32),
            pltpu.VMEM((80, 8, LANES), f32),
            pltpu.VMEM((80, 8, LANES), f32),
            pltpu.VMEM((LISTS, 2, 32, LANES), f32),
            pltpu.VMEM((LISTS, 4, 8, LANES), i32),
            pltpu.VMEM((4, 8 * TERM, LANES), f32),
            pltpu.VMEM((4, 8 * TERM, LANES), f32),
            pltpu.VMEM((2 * WIN, TERM, LANES), f32),
            pltpu.VMEM((2 * WIN, TERM, LANES), f32),
            pltpu.VMEM(((chunks + 1) * TERM, LANES), f32),
            pltpu.VMEM((LISTS, TERM, LANES), f32),
            pltpu.VMEM((LISTS, TERM, LANES), f32),
            pltpu.SemaphoreType.DMA((10,)),
            pltpu.SemaphoreType.DMA((2,)),
            pltpu.SemaphoreType.DMA((LISTS,)),
            pltpu.SemaphoreType.DMA((LISTS,)),
            pltpu.SemaphoreType.DMA((LISTS,)),
            pltpu.SemaphoreType.DMA((LISTS,)),
        ],
        compiler_params=pltpu.CompilerParams(
            collective_id=0,
            has_side_effects=True,
            vmem_limit_bytes=62 * 1024 * 1024,
        ),
    )(*args)
    return res, hess.reshape(nodes)


def solution(mesh):
    ndev = mesh.shape["dom"]

    def run(*args):
        return shards(ndev, *args)

    return jax.shard_map(
        run,
        mesh=mesh,
        in_specs=(
            P(None, "dom"),
            P(None, "dom"),
            P(None, "dom"),
            P("dom"),
            P("dom"),
            P(None, "dom"),
            P(None, "dom"),
            P(None, "dom"),
            P(None, "dom"),
            P("dom"),
            P("dom"),
        ),
        out_specs=(P(None, "dom"), P("dom")),
        check_vma=False,
    )
```

```python
import jax
import jax.numpy as jnp
from jax import lax
from jax.experimental import pallas as pl
from jax.experimental.pallas import tpu as pltpu
from jax.sharding import PartitionSpec as P

HOPS = 8
LISTS = 2 * HOPS
ELEM_BLOCK = 512
KAPPA = 0.5
PAIRS = ((0, 0), (1, 1), (2, 2), (0, 1), (0, 2), (1, 2))
LAYOUT = ((0, 3, 4), (3, 1, 5), (4, 5, 2))

LANES = 128
ROWS = 24
TAU, LAM, DLAM, DIR, ADJ = 0, 6, 7, 8, 16
FIELD_ROWS = tuple(range(0, 14)) + tuple(range(16, 22))
WIN = 3
TERM = 8

GATHER = lax.GatherDimensionNumbers(
    offset_dims=(),
    collapsed_slice_dims=(1,),
    start_index_map=(1,),
    operand_batching_dims=(0,),
    start_indices_batching_dims=(0,),
)


def pick_lanes(table, lane):
    return lax.gather(
        table,
        lane[:, :, None],
        GATHER,
        slice_sizes=(1, 1),
        mode=lax.GatherScatterMode.PROMISE_IN_BOUNDS,
    )


def list_offset(index):
    return jnp.where(index < HOPS, index + 1, HOPS - 1 - index)


def row_of(ref, row, height=8):
    return jnp.broadcast_to(ref[pl.ds(row, 1), :], (height, LANES))


def two_parts(values):
    high = values.astype(jnp.bfloat16).astype(jnp.float32)
    return jnp.concatenate([high, values - high], axis=0).astype(jnp.bfloat16)


def symmetric_product(left, right):
    prod = [
        [
            left[row][0] * right[LAYOUT[0][col]]
            + left[row][1] * right[LAYOUT[1][col]]
            + left[row][2] * right[LAYOUT[2][col]]
            for col in range(3)
        ]
        for row in range(3)
    ]
    return [prod[row][col] + prod[col][row] for row, col in PAIRS]


def make_kernel(ndev, nodes, elems):
    chunks = nodes // LANES
    nblocks = elems // ELEM_BLOCK
    groups = ELEM_BLOCK // LANES
    span = max(nblocks - 1, 1)
    window = WIN * LANES
    turns = LISTS // 2

    def kernel(
        stress_hbm,
        dir_hbm,
        adj_hbm,
        relax_hbm,
        rdir_hbm,
        conn_hbm,
        mass_hbm,
        adv_hbm,
        grad_hbm,
        send_hbm,
        count_ref,
        res_hbm,
        hess_hbm,
        stress,
        sdir,
        adjoint,
        relax,
        rdir,
        conn,
        mass,
        adv,
        grad,
        send,
        res,
        hess,
        fields,
        payload,
        ghosts,
        rolled0,
        rolled1,
        table0,
        table1,
        values,
        vel,
        vel8,
        gtable0,
        gtable1,
        merged0,
        merged1,
        index,
        rels,
        terms0,
        terms1,
        acc,
        gout,
        returned,
        in_sem,
        out_sem,
        send_sem,
        recv_sem,
        back_sem,
        ret_sem,
    ):
        me = lax.axis_index("dom")
        loads = [
            pltpu.make_async_copy(src, dst, in_sem.at[i])
            for i, (src, dst) in enumerate(
                [
                    (stress_hbm, stress),
                    (dir_hbm, sdir),
                    (adj_hbm, adjoint),
                    (relax_hbm, relax),
                    (rdir_hbm, rdir),
                    (send_hbm, send),
                    (conn_hbm, conn),
                    (grad_hbm, grad),
                    (mass_hbm, mass),
                    (adv_hbm, adv),
                ]
            )
        ]
        for load in loads:
            load.start()

        def inside(device):
            return (device >= 0) & (device < ndev)

        barrier = pltpu.get_barrier_semaphore()

        @pl.loop(0, LISTS)
        def _(k):
            target = me + list_offset(k)

            @pl.when(inside(target))
            def _():
                pl.semaphore_signal(
                    barrier, inc=1, device_id=(target,), device_id_type=pl.DeviceIdType.MESH
                )

        zeros = jnp.zeros((8, LANES), jnp.float32)
        lane = lax.broadcasted_iota(jnp.int32, (8, LANES), 1)
        sub = lax.broadcasted_iota(jnp.int32, (8, LANES), 0)
        upper = sub >= groups

        for load in loads[:6]:
            load.wait()

        for c in range(chunks):
            cut = pl.ds(c * LANES, LANES)
            for base in (TAU, DIR, ADJ):
                fields[pl.ds(c * ROWS + base, 8), :] = zeros
            fields[pl.ds(c * ROWS + TAU, 6), :] = 0.5 * KAPPA * stress[:, cut]
            fields[pl.ds(c * ROWS + LAM, 1), :] = relax[pl.ds(c, 1), :]
            fields[pl.ds(c * ROWS + DLAM, 1), :] = rdir[pl.ds(c, 1), :]
            fields[pl.ds(c * ROWS + DIR, 6), :] = sdir[:, cut]
            fields[pl.ds(c * ROWS + ADJ, 6), :] = adjoint[:, cut]
        for base in (TAU, DIR, ADJ):
            fields[pl.ds(chunks * ROWS + base, 8), :] = zeros

        def starts_of(pair):
            one = (2 * pair) * (nodes - window) // span
            two = (2 * pair + 1) * (nodes - window) // span
            return one, two

        def relative(pair, k):
            one, two = starts_of(pair)
            lists_one = (2 * pair) % LISTS
            node = conn[pl.ds(pair * 32 + k, 8, stride=4), :]
            start = jnp.where(upper, two, one)
            ghost0 = nodes + LANES * jnp.where(upper, lists_one + 1, lists_one) - window
            return node - jnp.where(node >= nodes, ghost0, start)

        count = count_ref[0]
        columns = lax.broadcasted_iota(jnp.int32, (LANES, LANES), 0).astype(jnp.bfloat16)
        one16 = jnp.ones((LANES, LANES), jnp.bfloat16)
        zero16 = jnp.zeros((LANES, LANES), jnp.bfloat16)
        contract = (((1,), (1,)), ((), ()))

        def factor(place_row):
            return jnp.where(columns == place_row, one16, zero16)

        def mark(pair):
            live = (pair * 8 + sub) * LANES + lane < count
            for k in range(4):
                rel = relative(pair, k)
                rels[pair, k] = rel
                index[pair, 0, pl.ds(8 * k, 8), :] = (rel & (LANES - 1)).astype(jnp.float32)
                index[pair, 1, pl.ds(8 * k, 8), :] = jnp.where(live, rel >> 7, -1).astype(
                    jnp.float32
                )

        for load in loads[6:7]:
            load.wait()

        @pl.loop(0, LISTS)
        def _(k):
            entry = row_of(send, k)
            place = entry & (LANES - 1)
            chunk = entry >> 7
            picked = [zeros, zeros, zeros]
            for c in range(chunks):
                here = chunk == c
                for t in range(3):
                    got = pick_lanes(fields[pl.ds(c * ROWS + 8 * t, 8), :], place)
                    picked[t] = jnp.where(here, got, picked[t])
            for t in range(3):
                payload[k, pl.ds(8 * t, 8), :] = picked[t]
            mark(k)

        first_up = jnp.minimum(HOPS, ndev - 1 - me)
        first_down = jnp.minimum(HOPS, me)
        pl.semaphore_wait(barrier, first_up + first_down)

        def push(k):
            target = me + list_offset(k)
            return pltpu.make_async_remote_copy(
                src_ref=payload.at[k],
                dst_ref=ghosts.at[k],
                send_sem=send_sem.at[k],
                recv_sem=recv_sem.at[k],
                device_id=(target,),
                device_id_type=pl.DeviceIdType.MESH,
            )

        def push_back(k):
            target = me - list_offset(k)
            return pltpu.make_async_remote_copy(
                src_ref=gout.at[k],
                dst_ref=returned.at[k],
                send_sem=back_sem.at[k],
                recv_sem=ret_sem.at[k],
                device_id=(target,),
                device_id_type=pl.DeviceIdType.MESH,
            )

        @pl.loop(0, LISTS)
        def _(k):
            @pl.when(inside(me + list_offset(k)))
            def _():
                push(k).start()

        for i in range(chunks + 1):
            acc[pl.ds(i * TERM, TERM), :] = zeros
        for i in range(LISTS):
            gout[i] = zeros
        for terms in (terms0, terms1):
            for k in range(4):
                for g in range(8):
                    terms[k, pl.ds(g * TERM, TERM), :] = zeros
        loads[7].wait()

        def weave(one, two):
            spent = [0, 0]
            parts = [one, two]
            while parts[0] is not None or parts[1] is not None:
                which = 0 if spent[0] <= spent[1] else 1
                if parts[which] is None:
                    which = 1 - which
                cost = next(parts[which], None)
                if cost is None:
                    parts[which] = None
                else:
                    spent[which] += cost

        def run(*parts):
            for part in parts:
                for _ in part:
                    pass

        def prepare(pair, rolled, table):
            for which, start in enumerate(starts_of(pair)):
                chunk0 = start // LANES
                shift = start % LANES
                keep = lane < LANES - shift
                for t in range(3):
                    turned = [
                        pltpu.roll(
                            fields[
                                pl.ds(pl.multiple_of((chunk0 + i) * ROWS + 8 * t, 8), 8), :
                            ],
                            (LANES - shift) % LANES,
                            1,
                        )
                        for i in range(WIN + 1)
                    ]
                    for i in range(WIN):
                        rolled[which, pl.ds(i * ROWS + 8 * t, 8), :] = jnp.where(
                            keep, turned[i], turned[i + 1]
                        )
            yield 50
            for n, row in enumerate(FIELD_ROWS):
                for i in range(WIN):
                    table[n * WIN + i] = jnp.where(
                        upper,
                        row_of(rolled.at[1], i * ROWS + row),
                        row_of(rolled.at[0], i * ROWS + row),
                    )
            yield 20

        def gather_owned(pair, table):
            for k in range(4):
                rel = rels[pair, k]
                place = rel & (LANES - 1)
                first = rel < LANES
                second = rel < 2 * LANES
                for n in range(20):
                    a, b, c = [pick_lanes(table[n * WIN + i], place) for i in range(WIN)]
                    values[pair, k * 20 + n] = jnp.where(first, a, jnp.where(second, b, c))
                    if n % 4 == 3:
                        yield 24
            for j in range(8):
                cut = pl.ds(pl.multiple_of((pair * 8 + j) * LANES, LANES), LANES)
                vel[pair, pl.ds(j * 8, 8), :] = grad[0:8, cut]
                vel8[pair, pl.ds(j, 1), :] = grad[8:9, cut]
            yield 8

        run(prepare(0, rolled0, table0))

        @pl.loop(0, turns)
        def _(i):
            weave(gather_owned(2 * i, table0), prepare(2 * i + 1, rolled1, table1))
            weave(
                gather_owned(2 * i + 1, table1),
                prepare(jnp.minimum(2 * i + 2, 2 * turns - 1), rolled0, table0),
            )

        for load in loads[8:]:
            load.wait()

        def gather_ghosts(pair, gtable, merged):
            listed = (2 * pair) % LISTS
            for n, row in enumerate(FIELD_ROWS):
                gtable[n] = jnp.where(
                    upper, row_of(ghosts.at[listed + 1], row), row_of(ghosts.at[listed], row)
                )
            yield 15
            for k in range(4):
                rel = rels[pair, k]
                place = rel & (LANES - 1)
                ghostly = rel >= window
                for n in range(20):
                    merged[k * 20 + n] = jnp.where(
                        ghostly, pick_lanes(gtable[n], place), values[pair, k * 20 + n]
                    )
                    if n % 10 == 9:
                        yield 20

        def algebra(pair, merged, terms):
            def got(k, n):
                return merged[k * 20 + n]

            lam_e = 0.25 * (got(0, 6) + got(1, 6) + got(2, 6) + got(3, 6))
            dlam4 = got(0, 7) + got(1, 7) + got(2, 7) + got(3, 7)
            grads = [vel[pair, pl.ds(i, 8, stride=8), :] for i in range(8)] + [vel8[pair]]
            tdir, gin, wsum, usum = [], [], [], []
            for k in range(4):
                tau = [got(k, c) for c in range(6)]
                t = [got(k, 8 + c) for c in range(6)]
                left_b = [
                    [tau[LAYOUT[r][c]] - grads[3 * r + c] for c in range(3)] for r in range(3)
                ]
                left_g = [
                    [left_b[r][c] + tau[LAYOUT[r][c]] for c in range(3)] for r in range(3)
                ]
                b_in = symmetric_product(left_b, tau)
                tdir.append(t)
                gin.append(symmetric_product(left_g, t))
                wsum.append([dlam4 * s for s in tau])
                usum.append([t[c] + dlam4 * b_in[c] for c in range(6)])
                yield 38
            score = zeros
            for a in range(4):
                mat, adm = [], []
                for b in range(4):
                    entry = 4 * a + b
                    at = (entry // 8) * (elems // 16) + pair * 64 + entry % 8
                    mat.append(mass[pl.ds(at, 8, stride=8), :])
                    adm.append(adv[pl.ds(at, 8, stride=8), :])
                for c in range(6):
                    g = adm[0] * tdir[0][c] + mat[0] * gin[0][c]
                    d = adm[0] * wsum[0][c] + mat[0] * usum[0][c]
                    for b in range(1, 4):
                        g = g + (adm[b] * tdir[b][c] + mat[b] * gin[b][c])
                        d = d + (adm[b] * wsum[b][c] + mat[b] * usum[b][c])
                    score = score + got(a, 14 + c) * g
                    terms[a, pl.ds(c, 8, stride=TERM), :] = d + lam_e * g
                    if c % 2 == 1:
                        yield 17
            score = 0.25 * score
            for a in range(4):
                terms[a, pl.ds(6, 8, stride=TERM), :] = score
            yield 2

        def scatter(pair, terms):
            listed = (2 * pair) % LISTS
            for which, start in enumerate(starts_of(pair)):
                lefts, rights = [], []
                for k in range(4):
                    for j in range(groups):
                        g = which * groups + j
                        part = two_parts(terms[k, pl.ds(g * TERM, TERM), :])
                        chunk = row_of(index.at[pair, 1], 8 * k + g, 16).astype(jnp.bfloat16)
                        place = row_of(index.at[pair, 0], 8 * k + g, 16).astype(jnp.bfloat16)
                        rights.append(factor(jnp.concatenate([place] * 8, axis=0)))
                        lefts.append(
                            jnp.concatenate(
                                [
                                    jnp.where(chunk == float(i), part, zero16[:16])
                                    for i in range(4)
                                ],
                                axis=0,
                            )
                        )
                    yield 32
                total = lax.dot_general(
                    jnp.concatenate(lefts, axis=1),
                    jnp.concatenate(rights, axis=1),
                    contract,
                    preferred_element_type=jnp.float32,
                )
                sums = [
                    total[16 * i : 16 * i + 8] + total[16 * i + 8 : 16 * i + 16]
                    for i in range(4)
                ]
                chunk0 = start // LANES
                shift = start % LANES
                turned = [pltpu.roll(sums[i], shift, 1) for i in range(WIN)]
                later = lane >= shift
                for i in range(WIN + 1):
                    if i == 0:
                        add = jnp.where(later, turned[0], 0.0)
                    elif i == WIN:
                        add = jnp.where(later, 0.0, turned[WIN - 1])
                    else:
                        add = jnp.where(later, turned[i], turned[i - 1])
                    at = pl.ds(pl.multiple_of((chunk0 + i) * TERM, TERM), TERM)
                    acc[at, :] = acc[at, :] + add
                gout[listed + which] = gout[listed + which] + sums[WIN]
                yield 10

        def both(one, two):
            yield from one
            yield from two

        def at_turn(step):
            return (step + turns // 2) % turns

        def await_ghosts(turn):
            for which in range(2):
                k = 2 * turn + which

                @pl.when(inside(me - list_offset(k)))
                def _():
                    push(k).wait_recv()

        def give_back(turn):
            for which in range(2):
                k = 2 * turn + which

                @pl.when(inside(me - list_offset(k)))
                def _():
                    push_back(k).start()

        first = at_turn(0)
        await_ghosts(first)
        run(gather_ghosts(first, gtable0, merged0))

        @pl.loop(0, turns)
        def _(step):
            turn = at_turn(step)
            after = at_turn(jnp.minimum(step + 1, turns - 1))
            before = at_turn(jnp.maximum(step - 1, 0))

            @pl.when(step < turns - 1)
            def _():
                await_ghosts(after)

            weave(
                gather_ghosts(turn + turns, gtable1, merged1),
                both(algebra(turn, merged0, terms0), scatter(before + turns, terms1)),
            )
            weave(
                gather_ghosts(after, gtable0, merged0),
                both(algebra(turn + turns, merged1, terms1), scatter(turn, terms0)),
            )

            @pl.when(step > 0)
            def _():
                give_back(before)

        last = at_turn(turns - 1)
        run(scatter(last + turns, terms1))
        give_back(last)

        total = jnp.zeros((chunks * 2 * TERM, LANES), jnp.float32)
        for step in range(turns):
            turn = (step + turns // 2) % turns
            if step % (turns // 2) == 0:

                @pl.loop(0, HOPS)
                def _(i):
                    k = 2 * turn + i

                    @pl.when(inside(me + list_offset(k)))
                    def _():
                        push_back(k).wait_recv()

            lefts, rights = [], []
            for k in (2 * turn, 2 * turn + 1):
                entry = row_of(send, k)
                part = two_parts(jnp.where(entry >= 0, returned[k], 0.0))
                entry16 = row_of(send, k, 16)
                chunk = (entry16 >> 7).astype(jnp.float32).astype(jnp.bfloat16)
                place = (entry16 & (LANES - 1)).astype(jnp.float32).astype(jnp.bfloat16)
                lefts.append(
                    jnp.concatenate(
                        [
                            jnp.where(chunk == float(i), part, zero16[:16])
                            for i in range(chunks)
                        ],
                        axis=0,
                    )
                )
                rights.append(factor(jnp.concatenate([place] * 8, axis=0)))
            total = total + lax.dot_general(
                jnp.concatenate(lefts, axis=1),
                jnp.concatenate(rights, axis=1),
                contract,
                preferred_element_type=jnp.float32,
            )
        for c in range(chunks):
            out = (
                acc[pl.ds(c * TERM, TERM), :]
                + total[16 * c : 16 * c + 8]
                + total[16 * c + 8 : 16 * c + 16]
            )
            res[:, pl.ds(c * LANES, LANES)] = out[0:6]
            hess[pl.ds(c, 1), :] = out[6:7]

        stores = [
            pltpu.make_async_copy(res, res_hbm, out_sem.at[0]),
            pltpu.make_async_copy(hess, hess_hbm, out_sem.at[1]),
        ]
        for store in stores:
            store.start()

        @pl.loop(0, LISTS)
        def _(k):
            @pl.when(inside(me + list_offset(k)))
            def _():
                push(k).wait_send()

            @pl.when(inside(me - list_offset(k)))
            def _():
                push_back(k).wait_send()

        for store in stores:
            store.wait()

    return kernel


def shards(
    ndev,
    stress,
    stress_dir,
    adjoint,
    relax,
    relax_dir,
    connect,
    mass_mat,
    adv_mat,
    vel_grad,
    send_list,
    elem_count,
):
    nodes = stress.shape[1]
    elems = connect.shape[1]
    chunks = nodes // LANES
    f32, i32 = jnp.float32, jnp.int32

    def by_groups(matrix, rows):
        split = matrix.reshape(-1, rows, elems // LANES, LANES)
        return split.transpose(0, 2, 1, 3).reshape(-1, LANES)

    args = (
        stress,
        stress_dir,
        adjoint,
        relax.reshape(chunks, LANES),
        relax_dir.reshape(chunks, LANES),
        by_groups(connect, 4),
        by_groups(mass_mat, 8),
        by_groups(adv_mat, 8),
        vel_grad,
        send_list.reshape(LISTS, LANES),
        elem_count,
    )
    hbm = pl.BlockSpec(memory_space=pl.ANY)
    res, hess = pl.pallas_call(
        make_kernel(ndev, nodes, elems),
        out_shape=(
            jax.ShapeDtypeStruct((6, nodes), f32),
            jax.ShapeDtypeStruct((chunks, LANES), f32),
        ),
        in_specs=[hbm] * 10 + [pl.BlockSpec(memory_space=pltpu.SMEM)],
        out_specs=(hbm, hbm),
        scratch_shapes=[
            pltpu.VMEM((6, nodes), f32),
            pltpu.VMEM((6, nodes), f32),
            pltpu.VMEM((6, nodes), f32),
            pltpu.VMEM((chunks, LANES), f32),
            pltpu.VMEM((chunks, LANES), f32),
            pltpu.VMEM((elems // 32, LANES), i32),
            pltpu.VMEM((elems // 8, LANES), f32),
            pltpu.VMEM((elems // 8, LANES), f32),
            pltpu.VMEM((9, elems), f32),
            pltpu.VMEM((LISTS, LANES), i32),
            pltpu.VMEM((6, nodes), f32),
            pltpu.VMEM((chunks, LANES), f32),
            pltpu.VMEM(((chunks + 1) * ROWS, LANES), f32),
            pltpu.VMEM((LISTS, ROWS, LANES), f32),
            pltpu.VMEM((LISTS, ROWS, LANES), f32),
            pltpu.VMEM((2, WIN * ROWS, LANES), f32),
            pltpu.VMEM((2, WIN * ROWS, LANES), f32),
            pltpu.VMEM((20 * WIN, 8, LANES), f32),
            pltpu.VMEM((20 * WIN, 8, LANES), f32),
            pltpu.VMEM((LISTS, 80, 8, LANES), f32),
            pltpu.VMEM((LISTS, 64, LANES), f32),
            pltpu.VMEM((LISTS, 8, LANES), f32),
            pltpu.VMEM((20, 8, LANES), f32),
            pltpu.VMEM((20, 8, LANES), f32),
            pltpu.VMEM((80, 8, LANES), f32),
            pltpu.VMEM((80, 8, LANES), f32),
            pltpu.VMEM((LISTS, 2, 32, LANES), f32),
            pltpu.VMEM((LISTS, 4, 8, LANES), i32),
            pltpu.VMEM((4, 8 * TERM, LANES), f32),
            pltpu.VMEM((4, 8 * TERM, LANES), f32),
            pltpu.VMEM(((chunks + 1) * TERM, LANES), f32),
            pltpu.VMEM((LISTS, TERM, LANES), f32),
            pltpu.VMEM((LISTS, TERM, LANES), f32),
            pltpu.SemaphoreType.DMA((10,)),
            pltpu.SemaphoreType.DMA((2,)),
            pltpu.SemaphoreType.DMA((LISTS,)),
            pltpu.SemaphoreType.DMA((LISTS,)),
            pltpu.SemaphoreType.DMA((LISTS,)),
            pltpu.SemaphoreType.DMA((LISTS,)),
        ],
        compiler_params=pltpu.CompilerParams(
            collective_id=0,
            has_side_effects=True,
            vmem_limit_bytes=62 * 1024 * 1024,
        ),
    )(*args)
    return res, hess.reshape(nodes)


def solution(mesh):
    ndev = mesh.shape["dom"]

    def run(*args):
        return shards(ndev, *args)

    return jax.shard_map(
        run,
        mesh=mesh,
        in_specs=(
            P(None, "dom"),
            P(None, "dom"),
            P(None, "dom"),
            P("dom"),
            P("dom"),
            P(None, "dom"),
            P(None, "dom"),
            P(None, "dom"),
            P(None, "dom"),
            P("dom"),
            P("dom"),
        ),
        out_specs=(P(None, "dom"), P("dom")),
        check_vma=False,
    )
```

```python
import jax
import jax.numpy as jnp
from jax import lax
from jax.experimental import pallas as pl
from jax.experimental.pallas import tpu as pltpu
from jax.sharding import PartitionSpec as P

HOPS = 8
LISTS = 2 * HOPS
ELEM_BLOCK = 512
KAPPA = 0.5
PAIRS = ((0, 0), (1, 1), (2, 2), (0, 1), (0, 2), (1, 2))
LAYOUT = ((0, 3, 4), (3, 1, 5), (4, 5, 2))

LANES = 128
ROWS = 24
TAU, LAM, DLAM, DIR, ADJ = 0, 6, 7, 8, 14
FIELDS = 20
FIELD_ROWS = tuple(range(FIELDS))
WIN = 3
TERM = 8

GATHER = lax.GatherDimensionNumbers(
    offset_dims=(),
    collapsed_slice_dims=(1,),
    start_index_map=(1,),
    operand_batching_dims=(0,),
    start_indices_batching_dims=(0,),
)


def pick_lanes(table, lane):
    return lax.gather(
        table,
        lane[:, :, None],
        GATHER,
        slice_sizes=(1, 1),
        mode=lax.GatherScatterMode.PROMISE_IN_BOUNDS,
    )


def list_offset(index):
    return jnp.where(index < HOPS, index + 1, HOPS - 1 - index)


def row_of(ref, row, height=8):
    return jnp.broadcast_to(ref[pl.ds(row, 1), :], (height, LANES))


def two_parts(values):
    high = values.astype(jnp.bfloat16).astype(jnp.float32)
    return jnp.concatenate([high, values - high], axis=0).astype(jnp.bfloat16)


def symmetric_product(left, right):
    prod = [
        [
            left[row][0] * right[LAYOUT[0][col]]
            + left[row][1] * right[LAYOUT[1][col]]
            + left[row][2] * right[LAYOUT[2][col]]
            for col in range(3)
        ]
        for row in range(3)
    ]
    return [prod[row][col] + prod[col][row] for row, col in PAIRS]


def make_kernel(ndev, nodes, elems):
    chunks = nodes // LANES
    nblocks = elems // ELEM_BLOCK
    groups = ELEM_BLOCK // LANES
    span = max(nblocks - 1, 1)
    window = WIN * LANES
    turns = LISTS // 2

    def kernel(
        stress_hbm,
        dir_hbm,
        adj_hbm,
        relax_hbm,
        rdir_hbm,
        conn_hbm,
        mass_hbm,
        adv_hbm,
        grad_hbm,
        send_hbm,
        count_ref,
        res_hbm,
        hess_hbm,
        stress,
        sdir,
        adjoint,
        relax,
        rdir,
        conn,
        mass,
        adv,
        grad,
        send,
        res,
        hess,
        fields,
        payload,
        ghosts,
        rolled0,
        rolled1,
        table0,
        table1,
        owned0,
        owned1,
        vel0,
        vel1,
        vel80,
        vel81,
        mvel0,
        mvel1,
        mvel80,
        mvel81,
        gtable0,
        gtable1,
        merged0,
        merged1,
        index,
        rels,
        terms0,
        terms1,
        acc,
        gout,
        returned,
        in_sem,
        out_sem,
        send_sem,
        recv_sem,
        back_sem,
        ret_sem,
    ):
        me = lax.axis_index("dom")
        loads = [
            pltpu.make_async_copy(src, dst, in_sem.at[i])
            for i, (src, dst) in enumerate(
                [
                    (stress_hbm, stress),
                    (dir_hbm, sdir),
                    (adj_hbm, adjoint),
                    (relax_hbm, relax),
                    (rdir_hbm, rdir),
                    (send_hbm, send),
                    (conn_hbm, conn),
                    (grad_hbm, grad),
                    (mass_hbm, mass),
                    (adv_hbm, adv),
                ]
            )
        ]
        for load in loads:
            load.start()

        def inside(device):
            return (device >= 0) & (device < ndev)

        barrier = pltpu.get_barrier_semaphore()

        @pl.loop(0, LISTS)
        def _(k):
            target = me + list_offset(k)

            @pl.when(inside(target))
            def _():
                pl.semaphore_signal(
                    barrier, inc=1, device_id=(target,), device_id_type=pl.DeviceIdType.MESH
                )

        zeros = jnp.zeros((8, LANES), jnp.float32)
        lane = lax.broadcasted_iota(jnp.int32, (8, LANES), 1)
        sub = lax.broadcasted_iota(jnp.int32, (8, LANES), 0)
        upper = sub >= groups

        for load in loads[:6]:
            load.wait()

        for c in range(chunks):
            cut = pl.ds(c * LANES, LANES)
            fields[pl.ds(c * ROWS + 16, 8), :] = zeros
            fields[pl.ds(c * ROWS + TAU, 6), :] = 0.5 * KAPPA * stress[:, cut]
            fields[pl.ds(c * ROWS + LAM, 1), :] = relax[pl.ds(c, 1), :]
            fields[pl.ds(c * ROWS + DLAM, 1), :] = rdir[pl.ds(c, 1), :]
            fields[pl.ds(c * ROWS + DIR, 6), :] = sdir[:, cut]
            fields[pl.ds(c * ROWS + ADJ, 6), :] = adjoint[:, cut]
        for base in (0, 8, 16):
            fields[pl.ds(chunks * ROWS + base, 8), :] = zeros

        def starts_of(pair):
            one = (2 * pair) * (nodes - window) // span
            two = (2 * pair + 1) * (nodes - window) // span
            return one, two

        def relative(pair, k):
            one, two = starts_of(pair)
            lists_one = (2 * pair) % LISTS
            node = conn[pl.ds(pair * 32 + k, 8, stride=4), :]
            start = jnp.where(upper, two, one)
            ghost0 = nodes + LANES * jnp.where(upper, lists_one + 1, lists_one) - window
            return node - jnp.where(node >= nodes, ghost0, start)

        count = count_ref[0]
        columns = lax.broadcasted_iota(jnp.int32, (LANES, LANES), 0).astype(jnp.bfloat16)
        one16 = jnp.ones((LANES, LANES), jnp.bfloat16)
        zero16 = jnp.zeros((LANES, LANES), jnp.bfloat16)
        contract = (((1,), (1,)), ((), ()))

        def factor(place_row):
            return jnp.where(columns == place_row, one16, zero16)

        def mark(pair):
            live = (pair * 8 + sub) * LANES + lane < count
            for k in range(4):
                rel = relative(pair, k)
                rels[pair, k] = rel
                index[pair, 0, pl.ds(8 * k, 8), :] = (rel & (LANES - 1)).astype(jnp.float32)
                index[pair, 1, pl.ds(8 * k, 8), :] = jnp.where(live, rel >> 7, -1).astype(
                    jnp.float32
                )

        for load in loads[6:7]:
            load.wait()

        @pl.loop(0, LISTS)
        def _(k):
            entry = row_of(send, k)
            place = entry & (LANES - 1)
            chunk = entry >> 7
            picked = [zeros, zeros, zeros]
            for c in range(chunks):
                here = chunk == c
                for t in range(3):
                    got = pick_lanes(fields[pl.ds(c * ROWS + 8 * t, 8), :], place)
                    picked[t] = jnp.where(here, got, picked[t])
            for t in range(3):
                payload[k, pl.ds(8 * t, 8), :] = picked[t]
            mark(k)

        first_up = jnp.minimum(HOPS, ndev - 1 - me)
        first_down = jnp.minimum(HOPS, me)
        pl.semaphore_wait(barrier, first_up + first_down)

        def push(k):
            target = me + list_offset(k)
            return pltpu.make_async_remote_copy(
                src_ref=payload.at[k, pl.ds(0, FIELDS)],
                dst_ref=ghosts.at[k, pl.ds(0, FIELDS)],
                send_sem=send_sem.at[k],
                recv_sem=recv_sem.at[k],
                device_id=(target,),
                device_id_type=pl.DeviceIdType.MESH,
            )

        def push_back(k):
            target = me - list_offset(k)
            return pltpu.make_async_remote_copy(
                src_ref=gout.at[k],
                dst_ref=returned.at[k],
                send_sem=back_sem.at[k],
                recv_sem=ret_sem.at[k],
                device_id=(target,),
                device_id_type=pl.DeviceIdType.MESH,
            )

        @pl.loop(0, LISTS)
        def _(i):
            k = (i + HOPS) % LISTS

            @pl.when(inside(me + list_offset(k)))
            def _():
                push(k).start()

        for i in range(chunks + 1):
            acc[pl.ds(i * TERM, TERM), :] = zeros
        for i in range(LISTS):
            gout[i] = zeros
        for terms in (terms0, terms1):
            for k in range(4):
                for g in range(8):
                    terms[k, pl.ds(g * TERM, TERM), :] = zeros
        loads[7].wait()

        def weave(one, two):
            spent = [0, 0]
            parts = [one, two]
            while parts[0] is not None or parts[1] is not None:
                which = 0 if spent[0] <= spent[1] else 1
                if parts[which] is None:
                    which = 1 - which
                cost = next(parts[which], None)
                if cost is None:
                    parts[which] = None
                else:
                    spent[which] += cost

        def run(*parts):
            for part in parts:
                for _ in part:
                    pass

        def prepare(pair, rolled, table):
            for which, start in enumerate(starts_of(pair)):
                chunk0 = start // LANES
                shift = start % LANES
                keep = lane < LANES - shift
                for t in range(3):
                    turned = [
                        pltpu.roll(
                            fields[
                                pl.ds(pl.multiple_of((chunk0 + i) * ROWS + 8 * t, 8), 8), :
                            ],
                            (LANES - shift) % LANES,
                            1,
                        )
                        for i in range(WIN + 1)
                    ]
                    for i in range(WIN):
                        rolled[which, pl.ds(i * ROWS + 8 * t, 8), :] = jnp.where(
                            keep, turned[i], turned[i + 1]
                        )
            yield 50
            for n, row in enumerate(FIELD_ROWS):
                for i in range(WIN):
                    table[n * WIN + i] = jnp.where(
                        upper,
                        row_of(rolled.at[1], i * ROWS + row),
                        row_of(rolled.at[0], i * ROWS + row),
                    )
            yield 20

        def gather_owned(pair, table, owned, vel, vel8):
            for k in range(4):
                rel = rels[pair, k]
                place = rel & (LANES - 1)
                first = rel < LANES
                second = rel < 2 * LANES
                for n in range(20):
                    a, b, c = [pick_lanes(table[n * WIN + i], place) for i in range(WIN)]
                    owned[k * 20 + n] = jnp.where(first, a, jnp.where(second, b, c))
                    if n % 4 == 3:
                        yield 24
            for j in range(8):
                cut = pl.ds(pl.multiple_of((pair * 8 + j) * LANES, LANES), LANES)
                vel[pl.ds(j * 8, 8), :] = grad[0:8, cut]
                vel8[pl.ds(j, 1), :] = grad[8:9, cut]
            yield 8

        def at_turn(step):
            return (step + turns // 2) % turns

        def await_ghosts(turn):
            for which in range(2):
                k = 2 * turn + which

                @pl.when(inside(me - list_offset(k)))
                def _():
                    push(k).wait_recv()

        first, second, third = at_turn(0), at_turn(1), at_turn(2)
        run(prepare(first, rolled0, table0), prepare(first + turns, rolled1, table1))
        run(gather_owned(first, table0, owned0, vel0, vel80), prepare(second, rolled0, table0))
        run(
            gather_owned(first + turns, table1, owned1, vel1, vel81),
            prepare(second + turns, rolled1, table1),
        )

        for load in loads[8:]:
            load.wait()

        def gather_ghosts(pair, gtable, owned, vel_in, vel8_in, merged, vel, vel8):
            listed = (2 * pair) % LISTS
            for n, row in enumerate(FIELD_ROWS):
                gtable[n] = jnp.where(
                    upper, row_of(ghosts.at[listed + 1], row), row_of(ghosts.at[listed], row)
                )
            vel[...] = vel_in[...]
            vel8[...] = vel8_in[...]
            yield 15
            for k in range(4):
                rel = rels[pair, k]
                place = rel & (LANES - 1)
                ghostly = rel >= window
                for n in range(20):
                    merged[k * 20 + n] = jnp.where(
                        ghostly, pick_lanes(gtable[n], place), owned[k * 20 + n]
                    )
                    if n % 10 == 9:
                        yield 20

        def algebra(pair, merged, vel_rows, vel8, terms):
            def got(k, n):
                return merged[k * 20 + n]

            lam_e = 0.25 * (got(0, 6) + got(1, 6) + got(2, 6) + got(3, 6))
            dlam4 = got(0, 7) + got(1, 7) + got(2, 7) + got(3, 7)
            vel = [vel_rows[pl.ds(i, 8, stride=8), :] for i in range(8)] + [vel8[...]]
            tdir, gin, wsum, usum = [], [], [], []
            for k in range(4):
                tau = [got(k, c) for c in range(6)]
                t = [got(k, 8 + c) for c in range(6)]
                left_b = [
                    [tau[LAYOUT[r][c]] - vel[3 * r + c] for c in range(3)] for r in range(3)
                ]
                left_g = [
                    [left_b[r][c] + tau[LAYOUT[r][c]] for c in range(3)] for r in range(3)
                ]
                b_in = symmetric_product(left_b, tau)
                tdir.append(t)
                gin.append(symmetric_product(left_g, t))
                wsum.append([dlam4 * s for s in tau])
                usum.append([t[c] + dlam4 * b_in[c] for c in range(6)])
                yield 38
            score = zeros
            for a in range(4):
                mat, adm = [], []
                for b in range(4):
                    entry = 4 * a + b
                    at = (entry // 8) * (elems // 16) + pair * 64 + entry % 8
                    mat.append(mass[pl.ds(at, 8, stride=8), :])
                    adm.append(adv[pl.ds(at, 8, stride=8), :])
                for c in range(6):
                    g = adm[0] * tdir[0][c] + mat[0] * gin[0][c]
                    d = adm[0] * wsum[0][c] + mat[0] * usum[0][c]
                    for b in range(1, 4):
                        g = g + (adm[b] * tdir[b][c] + mat[b] * gin[b][c])
                        d = d + (adm[b] * wsum[b][c] + mat[b] * usum[b][c])
                    score = score + got(a, 14 + c) * g
                    terms[a, pl.ds(c, 8, stride=TERM), :] = d + lam_e * g
                    if c % 2 == 1:
                        yield 17
            score = 0.25 * score
            for a in range(4):
                terms[a, pl.ds(6, 8, stride=TERM), :] = score
            yield 2

        def scatter(pair, terms):
            listed = (2 * pair) % LISTS
            for which, start in enumerate(starts_of(pair)):
                lefts, rights = [], []
                for k in range(4):
                    for j in range(groups):
                        g = which * groups + j
                        part = two_parts(terms[k, pl.ds(g * TERM, TERM), :])
                        chunk = row_of(index.at[pair, 1], 8 * k + g, 16).astype(jnp.bfloat16)
                        place = row_of(index.at[pair, 0], 8 * k + g, 16).astype(jnp.bfloat16)
                        rights.append(factor(jnp.concatenate([place] * 8, axis=0)))
                        lefts.append(
                            jnp.concatenate(
                                [
                                    jnp.where(chunk == float(i), part, zero16[:16])
                                    for i in range(4)
                                ],
                                axis=0,
                            )
                        )
                    yield 32
                total = lax.dot_general(
                    jnp.concatenate(lefts, axis=1),
                    jnp.concatenate(rights, axis=1),
                    contract,
                    preferred_element_type=jnp.float32,
                )
                sums = [
                    total[16 * i : 16 * i + 8] + total[16 * i + 8 : 16 * i + 16]
                    for i in range(4)
                ]
                chunk0 = start // LANES
                shift = start % LANES
                turned = [pltpu.roll(sums[i], shift, 1) for i in range(WIN)]
                later = lane >= shift
                for i in range(WIN + 1):
                    if i == 0:
                        add = jnp.where(later, turned[0], 0.0)
                    elif i == WIN:
                        add = jnp.where(later, 0.0, turned[WIN - 1])
                    else:
                        add = jnp.where(later, turned[i], turned[i - 1])
                    at = pl.ds(pl.multiple_of((chunk0 + i) * TERM, TERM), TERM)
                    acc[at, :] = acc[at, :] + add
                gout[listed + which] = gout[listed + which] + sums[WIN]
                yield 10

        def both(one, two):
            yield from one
            yield from two

        def give_back(turn):
            for which in range(2):
                k = 2 * turn + which

                @pl.when(inside(me - list_offset(k)))
                def _():
                    push_back(k).start()

        def merge(turn, half):
            if half == 0:
                return gather_ghosts(
                    turn, gtable0, owned0, vel0, vel80, merged0, mvel0, mvel80
                )
            return gather_ghosts(
                turn + turns, gtable1, owned1, vel1, vel81, merged1, mvel1, mvel81
            )

        def look_ahead(turn, after, half):
            if half == 0:
                yield from gather_owned(turn, table0, owned0, vel0, vel80)
                yield from prepare(after, rolled0, table0)
            else:
                yield from gather_owned(turn + turns, table1, owned1, vel1, vel81)
                yield from prepare(after + turns, rolled1, table1)

        await_ghosts(first)
        run(merge(first, 0), look_ahead(second, third, 0))

        @pl.loop(0, turns)
        def _(step):
            before = at_turn(jnp.maximum(step - 1, 0))
            turn = at_turn(step)
            one, two, three = [
                at_turn(jnp.minimum(step + ahead, turns - 1)) for ahead in (1, 2, 3)
            ]

            @pl.when(step < turns - 1)
            def _():
                await_ghosts(one)

            weave(
                both(merge(turn, 1), look_ahead(one, two, 1)),
                both(
                    algebra(turn, merged0, mvel0, mvel80, terms0),
                    scatter(before + turns, terms1),
                ),
            )
            weave(
                both(merge(one, 0), look_ahead(two, three, 0)),
                both(
                    algebra(turn + turns, merged1, mvel1, mvel81, terms1),
                    scatter(turn, terms0),
                ),
            )

            @pl.when(step > 0)
            def _():
                give_back(before)

        last = at_turn(turns - 1)
        run(scatter(last + turns, terms1))
        give_back(last)

        total = jnp.zeros((chunks * 2 * TERM, LANES), jnp.float32)
        for step in range(turns):
            turn = (step + turns // 2) % turns
            if step % (turns // 2) == 0:

                @pl.loop(0, HOPS)
                def _(i):
                    k = 2 * turn + i

                    @pl.when(inside(me + list_offset(k)))
                    def _():
                        push_back(k).wait_recv()

            lefts, rights = [], []
            for k in (2 * turn, 2 * turn + 1):
                entry = row_of(send, k)
                part = two_parts(jnp.where(entry >= 0, returned[k], 0.0))
                entry16 = row_of(send, k, 16)
                chunk = (entry16 >> 7).astype(jnp.float32).astype(jnp.bfloat16)
                place = (entry16 & (LANES - 1)).astype(jnp.float32).astype(jnp.bfloat16)
                lefts.append(
                    jnp.concatenate(
                        [
                            jnp.where(chunk == float(i), part, zero16[:16])
                            for i in range(chunks)
                        ],
                        axis=0,
                    )
                )
                rights.append(factor(jnp.concatenate([place] * 8, axis=0)))
            total = total + lax.dot_general(
                jnp.concatenate(lefts, axis=1),
                jnp.concatenate(rights, axis=1),
                contract,
                preferred_element_type=jnp.float32,
            )
        for c in range(chunks):
            out = (
                acc[pl.ds(c * TERM, TERM), :]
                + total[16 * c : 16 * c + 8]
                + total[16 * c + 8 : 16 * c + 16]
            )
            res[:, pl.ds(c * LANES, LANES)] = out[0:6]
            hess[pl.ds(c, 1), :] = out[6:7]

        stores = [
            pltpu.make_async_copy(res, res_hbm, out_sem.at[0]),
            pltpu.make_async_copy(hess, hess_hbm, out_sem.at[1]),
        ]
        for store in stores:
            store.start()

        @pl.loop(0, LISTS)
        def _(k):
            @pl.when(inside(me + list_offset(k)))
            def _():
                push(k).wait_send()

            @pl.when(inside(me - list_offset(k)))
            def _():
                push_back(k).wait_send()

        for store in stores:
            store.wait()

    return kernel


def shards(
    ndev,
    stress,
    stress_dir,
    adjoint,
    relax,
    relax_dir,
    connect,
    mass_mat,
    adv_mat,
    vel_grad,
    send_list,
    elem_count,
):
    nodes = stress.shape[1]
    elems = connect.shape[1]
    chunks = nodes // LANES
    f32, i32 = jnp.float32, jnp.int32

    def by_groups(matrix, rows):
        split = matrix.reshape(-1, rows, elems // LANES, LANES)
        return split.transpose(0, 2, 1, 3).reshape(-1, LANES)

    args = (
        stress,
        stress_dir,
        adjoint,
        relax.reshape(chunks, LANES),
        relax_dir.reshape(chunks, LANES),
        by_groups(connect, 4),
        by_groups(mass_mat, 8),
        by_groups(adv_mat, 8),
        vel_grad,
        send_list.reshape(LISTS, LANES),
        elem_count,
    )
    hbm = pl.BlockSpec(memory_space=pl.ANY)
    res, hess = pl.pallas_call(
        make_kernel(ndev, nodes, elems),
        out_shape=(
            jax.ShapeDtypeStruct((6, nodes), f32),
            jax.ShapeDtypeStruct((chunks, LANES), f32),
        ),
        in_specs=[hbm] * 10 + [pl.BlockSpec(memory_space=pltpu.SMEM)],
        out_specs=(hbm, hbm),
        scratch_shapes=[
            pltpu.VMEM((6, nodes), f32),
            pltpu.VMEM((6, nodes), f32),
            pltpu.VMEM((6, nodes), f32),
            pltpu.VMEM((chunks, LANES), f32),
            pltpu.VMEM((chunks, LANES), f32),
            pltpu.VMEM((elems // 32, LANES), i32),
            pltpu.VMEM((elems // 8, LANES), f32),
            pltpu.VMEM((elems // 8, LANES), f32),
            pltpu.VMEM((9, elems), f32),
            pltpu.VMEM((LISTS, LANES), i32),
            pltpu.VMEM((6, nodes), f32),
            pltpu.VMEM((chunks, LANES), f32),
            pltpu.VMEM(((chunks + 1) * ROWS, LANES), f32),
            pltpu.VMEM((LISTS, ROWS, LANES), f32),
            pltpu.VMEM((LISTS, ROWS, LANES), f32),
            pltpu.VMEM((2, WIN * ROWS, LANES), f32),
            pltpu.VMEM((2, WIN * ROWS, LANES), f32),
            pltpu.VMEM((20 * WIN, 8, LANES), f32),
            pltpu.VMEM((20 * WIN, 8, LANES), f32),
            pltpu.VMEM((80, 8, LANES), f32),
            pltpu.VMEM((80, 8, LANES), f32),
            pltpu.VMEM((64, LANES), f32),
            pltpu.VMEM((64, LANES), f32),
            pltpu.VMEM((8, LANES), f32),
            pltpu.VMEM((8, LANES), f32),
            pltpu.VMEM((64, LANES), f32),
            pltpu.VMEM((64, LANES), f32),
            pltpu.VMEM((8, LANES), f32),
            pltpu.VMEM((8, LANES), f32),
            pltpu.VMEM((20, 8, LANES), f32),
            pltpu.VMEM((20, 8, LANES), f32),
            pltpu.VMEM((80, 8, LANES), f32),
            pltpu.VMEM((80, 8, LANES), f32),
            pltpu.VMEM((LISTS, 2, 32, LANES), f32),
            pltpu.VMEM((LISTS, 4, 8, LANES), i32),
            pltpu.VMEM((4, 8 * TERM, LANES), f32),
            pltpu.VMEM((4, 8 * TERM, LANES), f32),
            pltpu.VMEM(((chunks + 1) * TERM, LANES), f32),
            pltpu.VMEM((LISTS, TERM, LANES), f32),
            pltpu.VMEM((LISTS, TERM, LANES), f32),
            pltpu.SemaphoreType.DMA((10,)),
            pltpu.SemaphoreType.DMA((2,)),
            pltpu.SemaphoreType.DMA((LISTS,)),
            pltpu.SemaphoreType.DMA((LISTS,)),
            pltpu.SemaphoreType.DMA((LISTS,)),
            pltpu.SemaphoreType.DMA((LISTS,)),
        ],
        compiler_params=pltpu.CompilerParams(
            collective_id=0,
            has_side_effects=True,
            vmem_limit_bytes=62 * 1024 * 1024,
        ),
    )(*args)
    return res, hess.reshape(nodes)


def solution(mesh):
    ndev = mesh.shape["dom"]

    def run(*args):
        return shards(ndev, *args)

    return jax.shard_map(
        run,
        mesh=mesh,
        in_specs=(
            P(None, "dom"),
            P(None, "dom"),
            P(None, "dom"),
            P("dom"),
            P("dom"),
            P(None, "dom"),
            P(None, "dom"),
            P(None, "dom"),
            P(None, "dom"),
            P("dom"),
            P("dom"),
        ),
        out_specs=(P(None, "dom"), P("dom")),
        check_vma=False,
    )
```

```python
import jax
import jax.numpy as jnp
from jax import lax
from jax.experimental import pallas as pl
from jax.experimental.pallas import tpu as pltpu
from jax.sharding import PartitionSpec as P

HOPS = 8
LISTS = 2 * HOPS
ELEM_BLOCK = 512
KAPPA = 0.5
PAIRS = ((0, 0), (1, 1), (2, 2), (0, 1), (0, 2), (1, 2))
LAYOUT = ((0, 3, 4), (3, 1, 5), (4, 5, 2))

LANES = 128
ROWS = 24
TAU, LAM, DLAM, DIR, ADJ = 0, 6, 7, 8, 14
FIELDS = 20
FIELD_ROWS = tuple(range(FIELDS))
WIN = 3
TERM = 8

GATHER = lax.GatherDimensionNumbers(
    offset_dims=(),
    collapsed_slice_dims=(1,),
    start_index_map=(1,),
    operand_batching_dims=(0,),
    start_indices_batching_dims=(0,),
)


def pick_lanes(table, lane):
    return lax.gather(
        table,
        lane[:, :, None],
        GATHER,
        slice_sizes=(1, 1),
        mode=lax.GatherScatterMode.PROMISE_IN_BOUNDS,
    )


def list_offset(index):
    return jnp.where(index < HOPS, index + 1, HOPS - 1 - index)


def row_of(ref, row, height=8):
    return jnp.broadcast_to(ref[pl.ds(row, 1), :], (height, LANES))


def two_parts(values):
    high = values.astype(jnp.bfloat16).astype(jnp.float32)
    return jnp.concatenate([high, values - high], axis=0).astype(jnp.bfloat16)


def symmetric_product(left, right):
    prod = [
        [
            left[row][0] * right[LAYOUT[0][col]]
            + left[row][1] * right[LAYOUT[1][col]]
            + left[row][2] * right[LAYOUT[2][col]]
            for col in range(3)
        ]
        for row in range(3)
    ]
    return [prod[row][col] + prod[col][row] for row, col in PAIRS]


def make_kernel(ndev, nodes, elems):
    chunks = nodes // LANES
    nblocks = elems // ELEM_BLOCK
    groups = ELEM_BLOCK // LANES
    span = max(nblocks - 1, 1)
    window = WIN * LANES
    turns = LISTS // 2

    def kernel(
        stress_hbm,
        dir_hbm,
        adj_hbm,
        relax_hbm,
        rdir_hbm,
        conn_hbm,
        mass_hbm,
        adv_hbm,
        grad_hbm,
        send_hbm,
        count_ref,
        acc_hbm,
        returned,
        stress,
        sdir,
        adjoint,
        relax,
        rdir,
        conn,
        mass,
        adv,
        grad,
        send,
        fields,
        payload,
        ghosts,
        rolled0,
        rolled1,
        table0,
        table1,
        owned0,
        owned1,
        vel0,
        vel1,
        vel80,
        vel81,
        mvel0,
        mvel1,
        mvel80,
        mvel81,
        gtable0,
        gtable1,
        merged0,
        merged1,
        index,
        rels,
        terms0,
        terms1,
        acc,
        gout,
        in_sem,
        out_sem,
        send_sem,
        recv_sem,
        back_sem,
        ret_sem,
    ):
        me = lax.axis_index("dom")
        loads = [
            pltpu.make_async_copy(src, dst, in_sem.at[i])
            for i, (src, dst) in enumerate(
                [
                    (stress_hbm, stress),
                    (dir_hbm, sdir),
                    (adj_hbm, adjoint),
                    (relax_hbm, relax),
                    (rdir_hbm, rdir),
                    (send_hbm, send),
                    (conn_hbm, conn),
                    (grad_hbm, grad),
                    (mass_hbm, mass),
                    (adv_hbm, adv),
                ]
            )
        ]
        for load in loads:
            load.start()

        def inside(device):
            return (device >= 0) & (device < ndev)

        barrier = pltpu.get_barrier_semaphore()

        @pl.loop(0, LISTS)
        def _(k):
            target = me + list_offset(k)

            @pl.when(inside(target))
            def _():
                pl.semaphore_signal(
                    barrier, inc=1, device_id=(target,), device_id_type=pl.DeviceIdType.MESH
                )

        zeros = jnp.zeros((8, LANES), jnp.float32)
        lane = lax.broadcasted_iota(jnp.int32, (8, LANES), 1)
        sub = lax.broadcasted_iota(jnp.int32, (8, LANES), 0)
        upper = sub >= groups

        for load in loads[:6]:
            load.wait()

        for c in range(chunks):
            cut = pl.ds(c * LANES, LANES)
            fields[pl.ds(c * ROWS + 16, 8), :] = zeros
            fields[pl.ds(c * ROWS + TAU, 6), :] = 0.5 * KAPPA * stress[:, cut]
            fields[pl.ds(c * ROWS + LAM, 1), :] = relax[pl.ds(c, 1), :]
            fields[pl.ds(c * ROWS + DLAM, 1), :] = rdir[pl.ds(c, 1), :]
            fields[pl.ds(c * ROWS + DIR, 6), :] = sdir[:, cut]
            fields[pl.ds(c * ROWS + ADJ, 6), :] = adjoint[:, cut]
        for base in (0, 8, 16):
            fields[pl.ds(chunks * ROWS + base, 8), :] = zeros

        def starts_of(pair):
            one = (2 * pair) * (nodes - window) // span
            two = (2 * pair + 1) * (nodes - window) // span
            return one, two

        def relative(pair, k):
            one, two = starts_of(pair)
            lists_one = (2 * pair) % LISTS
            node = conn[pl.ds(pair * 32 + k, 8, stride=4), :]
            start = jnp.where(upper, two, one)
            ghost0 = nodes + LANES * jnp.where(upper, lists_one + 1, lists_one) - window
            return node - jnp.where(node >= nodes, ghost0, start)

        count = count_ref[0]
        columns = lax.broadcasted_iota(jnp.int32, (LANES, LANES), 0).astype(jnp.bfloat16)
        one16 = jnp.ones((LANES, LANES), jnp.bfloat16)
        zero16 = jnp.zeros((LANES, LANES), jnp.bfloat16)
        contract = (((1,), (1,)), ((), ()))

        def factor(place_row):
            return jnp.where(columns == place_row, one16, zero16)

        def mark(pair):
            live = (pair * 8 + sub) * LANES + lane < count
            for k in range(4):
                rel = relative(pair, k)
                rels[pair, k] = rel
                index[pair, 0, pl.ds(8 * k, 8), :] = (rel & (LANES - 1)).astype(jnp.float32)
                index[pair, 1, pl.ds(8 * k, 8), :] = jnp.where(live, rel >> 7, -1).astype(
                    jnp.float32
                )

        for load in loads[6:7]:
            load.wait()

        @pl.loop(0, LISTS)
        def _(k):
            entry = row_of(send, k)
            place = entry & (LANES - 1)
            chunk = entry >> 7
            picked = [zeros, zeros, zeros]
            for c in range(chunks):
                here = chunk == c
                for t in range(3):
                    got = pick_lanes(fields[pl.ds(c * ROWS + 8 * t, 8), :], place)
                    picked[t] = jnp.where(here, got, picked[t])
            for t in range(3):
                payload[k, pl.ds(8 * t, 8), :] = picked[t]
            mark(k)

        first_up = jnp.minimum(HOPS, ndev - 1 - me)
        first_down = jnp.minimum(HOPS, me)
        pl.semaphore_wait(barrier, first_up + first_down)

        def push(k):
            target = me + list_offset(k)
            return pltpu.make_async_remote_copy(
                src_ref=payload.at[k, pl.ds(0, FIELDS)],
                dst_ref=ghosts.at[k, pl.ds(0, FIELDS)],
                send_sem=send_sem.at[k],
                recv_sem=recv_sem.at[k],
                device_id=(target,),
                device_id_type=pl.DeviceIdType.MESH,
            )

        def push_back(k):
            target = me - list_offset(k)
            return pltpu.make_async_remote_copy(
                src_ref=gout.at[k],
                dst_ref=returned.at[k],
                send_sem=back_sem.at[k],
                recv_sem=ret_sem.at[k],
                device_id=(target,),
                device_id_type=pl.DeviceIdType.MESH,
            )

        @pl.loop(0, LISTS)
        def _(i):
            k = (i + HOPS) % LISTS

            @pl.when(inside(me + list_offset(k)))
            def _():
                push(k).start()

        for i in range(chunks + 1):
            acc[pl.ds(i * TERM, TERM), :] = zeros
        for i in range(LISTS):
            gout[i] = zeros
        for terms in (terms0, terms1):
            for k in range(4):
                for g in range(8):
                    terms[k, pl.ds(g * TERM, TERM), :] = zeros
        loads[7].wait()

        def weave(one, two):
            spent = [0, 0]
            parts = [one, two]
            while parts[0] is not None or parts[1] is not None:
                which = 0 if spent[0] <= spent[1] else 1
                if parts[which] is None:
                    which = 1 - which
                cost = next(parts[which], None)
                if cost is None:
                    parts[which] = None
                else:
                    spent[which] += cost

        def run(*parts):
            for part in parts:
                for _ in part:
                    pass

        def prepare(pair, rolled, table):
            for which, start in enumerate(starts_of(pair)):
                chunk0 = start // LANES
                shift = start % LANES
                keep = lane < LANES - shift
                for t in range(3):
                    turned = [
                        pltpu.roll(
                            fields[
                                pl.ds(pl.multiple_of((chunk0 + i) * ROWS + 8 * t, 8), 8), :
                            ],
                            (LANES - shift) % LANES,
                            1,
                        )
                        for i in range(WIN + 1)
                    ]
                    for i in range(WIN):
                        rolled[which, pl.ds(i * ROWS + 8 * t, 8), :] = jnp.where(
                            keep, turned[i], turned[i + 1]
                        )
            yield 50
            for n, row in enumerate(FIELD_ROWS):
                for i in range(WIN):
                    table[n * WIN + i] = jnp.where(
                        upper,
                        row_of(rolled.at[1], i * ROWS + row),
                        row_of(rolled.at[0], i * ROWS + row),
                    )
            yield 20

        def gather_owned(pair, table, owned, vel, vel8):
            for k in range(4):
                rel = rels[pair, k]
                place = rel & (LANES - 1)
                first = rel < LANES
                second = rel < 2 * LANES
                for n in range(20):
                    a, b, c = [pick_lanes(table[n * WIN + i], place) for i in range(WIN)]
                    owned[k * 20 + n] = jnp.where(first, a, jnp.where(second, b, c))
                    if n % 4 == 3:
                        yield 24
            for j in range(8):
                cut = pl.ds(pl.multiple_of((pair * 8 + j) * LANES, LANES), LANES)
                vel[pl.ds(j * 8, 8), :] = grad[0:8, cut]
                vel8[pl.ds(j, 1), :] = grad[8:9, cut]
            yield 8

        def at_turn(step):
            return (step + turns // 2) % turns

        def await_ghosts(turn):
            for which in range(2):
                k = 2 * turn + which

                @pl.when(inside(me - list_offset(k)))
                def _():
                    push(k).wait_recv()

        first, second, third = at_turn(0), at_turn(1), at_turn(2)
        run(prepare(first, rolled0, table0), prepare(first + turns, rolled1, table1))
        run(gather_owned(first, table0, owned0, vel0, vel80), prepare(second, rolled0, table0))
        run(
            gather_owned(first + turns, table1, owned1, vel1, vel81),
            prepare(second + turns, rolled1, table1),
        )

        for load in loads[8:]:
            load.wait()

        def gather_ghosts(pair, gtable, owned, vel_in, vel8_in, merged, vel, vel8):
            listed = (2 * pair) % LISTS
            for n, row in enumerate(FIELD_ROWS):
                gtable[n] = jnp.where(
                    upper, row_of(ghosts.at[listed + 1], row), row_of(ghosts.at[listed], row)
                )
            vel[...] = vel_in[...]
            vel8[...] = vel8_in[...]
            yield 15
            for k in range(4):
                rel = rels[pair, k]
                place = rel & (LANES - 1)
                ghostly = rel >= window
                for n in range(20):
                    merged[k * 20 + n] = jnp.where(
                        ghostly, pick_lanes(gtable[n], place), owned[k * 20 + n]
                    )
                    if n % 10 == 9:
                        yield 20

        def algebra(pair, merged, vel_rows, vel8, terms):
            def got(k, n):
                return merged[k * 20 + n]

            lam_e = 0.25 * (got(0, 6) + got(1, 6) + got(2, 6) + got(3, 6))
            dlam4 = got(0, 7) + got(1, 7) + got(2, 7) + got(3, 7)
            vel = [vel_rows[pl.ds(i, 8, stride=8), :] for i in range(8)] + [vel8[...]]
            tdir, gin, wsum, usum = [], [], [], []
            for k in range(4):
                tau = [got(k, c) for c in range(6)]
                t = [got(k, 8 + c) for c in range(6)]
                left_b = [
                    [tau[LAYOUT[r][c]] - vel[3 * r + c] for c in range(3)] for r in range(3)
                ]
                left_g = [
                    [left_b[r][c] + tau[LAYOUT[r][c]] for c in range(3)] for r in range(3)
                ]
                b_in = symmetric_product(left_b, tau)
                tdir.append(t)
                gin.append(symmetric_product(left_g, t))
                wsum.append([dlam4 * s for s in tau])
                usum.append([t[c] + dlam4 * b_in[c] for c in range(6)])
                yield 38
            score = zeros
            for a in range(4):
                mat, adm = [], []
                for b in range(4):
                    entry = 4 * a + b
                    at = (entry // 8) * (elems // 16) + pair * 64 + entry % 8
                    mat.append(mass[pl.ds(at, 8, stride=8), :])
                    adm.append(adv[pl.ds(at, 8, stride=8), :])
                for c in range(6):
                    g = adm[0] * tdir[0][c] + mat[0] * gin[0][c]
                    d = adm[0] * wsum[0][c] + mat[0] * usum[0][c]
                    for b in range(1, 4):
                        g = g + (adm[b] * tdir[b][c] + mat[b] * gin[b][c])
                        d = d + (adm[b] * wsum[b][c] + mat[b] * usum[b][c])
                    score = score + got(a, 14 + c) * g
                    terms[a, pl.ds(c, 8, stride=TERM), :] = d + lam_e * g
                    if c % 2 == 1:
                        yield 17
            score = 0.25 * score
            for a in range(4):
                terms[a, pl.ds(6, 8, stride=TERM), :] = score
            yield 2

        def scatter(pair, terms):
            listed = (2 * pair) % LISTS
            for which, start in enumerate(starts_of(pair)):
                lefts, rights = [], []
                for k in range(4):
                    for j in range(groups):
                        g = which * groups + j
                        part = two_parts(terms[k, pl.ds(g * TERM, TERM), :])
                        chunk = row_of(index.at[pair, 1], 8 * k + g, 16).astype(jnp.bfloat16)
                        place = row_of(index.at[pair, 0], 8 * k + g, 16).astype(jnp.bfloat16)
                        rights.append(factor(jnp.concatenate([place] * 8, axis=0)))
                        lefts.append(
                            jnp.concatenate(
                                [
                                    jnp.where(chunk == float(i), part, zero16[:16])
                                    for i in range(4)
                                ],
                                axis=0,
                            )
                        )
                    yield 32
                total = lax.dot_general(
                    jnp.concatenate(lefts, axis=1),
                    jnp.concatenate(rights, axis=1),
                    contract,
                    preferred_element_type=jnp.float32,
                )
                sums = [
                    total[16 * i : 16 * i + 8] + total[16 * i + 8 : 16 * i + 16]
                    for i in range(4)
                ]
                chunk0 = start // LANES
                shift = start % LANES
                turned = [pltpu.roll(sums[i], shift, 1) for i in range(WIN)]
                later = lane >= shift
                for i in range(WIN + 1):
                    if i == 0:
                        add = jnp.where(later, turned[0], 0.0)
                    elif i == WIN:
                        add = jnp.where(later, 0.0, turned[WIN - 1])
                    else:
                        add = jnp.where(later, turned[i], turned[i - 1])
                    at = pl.ds(pl.multiple_of((chunk0 + i) * TERM, TERM), TERM)
                    acc[at, :] = acc[at, :] + add
                gout[listed + which] = gout[listed + which] + sums[WIN]
                yield 10

        def both(one, two):
            yield from one
            yield from two

        def give_back(turn):
            for which in range(2):
                k = 2 * turn + which

                @pl.when(inside(me - list_offset(k)))
                def _():
                    push_back(k).start()

        def merge(turn, half):
            if half == 0:
                return gather_ghosts(
                    turn, gtable0, owned0, vel0, vel80, merged0, mvel0, mvel80
                )
            return gather_ghosts(
                turn + turns, gtable1, owned1, vel1, vel81, merged1, mvel1, mvel81
            )

        def look_ahead(turn, after, half):
            if half == 0:
                yield from gather_owned(turn, table0, owned0, vel0, vel80)
                yield from prepare(after, rolled0, table0)
            else:
                yield from gather_owned(turn + turns, table1, owned1, vel1, vel81)
                yield from prepare(after + turns, rolled1, table1)

        await_ghosts(first)
        run(merge(first, 0), look_ahead(second, third, 0))

        @pl.loop(0, turns)
        def _(step):
            before = at_turn(jnp.maximum(step - 1, 0))
            turn = at_turn(step)
            one, two, three = [
                at_turn(jnp.minimum(step + ahead, turns - 1)) for ahead in (1, 2, 3)
            ]

            @pl.when(step < turns - 1)
            def _():
                await_ghosts(one)

            weave(
                both(merge(turn, 1), look_ahead(one, two, 1)),
                both(
                    algebra(turn, merged0, mvel0, mvel80, terms0),
                    scatter(before + turns, terms1),
                ),
            )
            weave(
                both(merge(one, 0), look_ahead(two, three, 0)),
                both(
                    algebra(turn + turns, merged1, mvel1, mvel81, terms1),
                    scatter(turn, terms0),
                ),
            )

            @pl.when(step > 0)
            def _():
                give_back(before)

        last = at_turn(turns - 1)
        run(scatter(last + turns, terms1))
        give_back(last)

        store = pltpu.make_async_copy(acc.at[pl.ds(0, chunks * TERM)], acc_hbm, out_sem.at[0])
        store.start()

        @pl.loop(0, LISTS)
        def _(k):
            @pl.when(inside(me + list_offset(k)))
            def _():
                push(k).wait_send()
                push_back(k).wait_recv()

            @pl.when(inside(me - list_offset(k)))
            def _():
                push_back(k).wait_send()

        store.wait()

    return kernel


def finish(acc, returned, send, res, hess):
    chunks = hess.shape[0]
    columns = lax.broadcasted_iota(jnp.int32, (LANES, LANES), 0).astype(jnp.bfloat16)
    one16 = jnp.ones((LANES, LANES), jnp.bfloat16)
    zero16 = jnp.zeros((LANES, LANES), jnp.bfloat16)
    total = jnp.zeros((chunks * 2 * TERM, LANES), jnp.float32)
    for pairing in range(LISTS // 2):
        lefts, rights = [], []
        for k in (2 * pairing, 2 * pairing + 1):
            entry = row_of(send, k)
            part = two_parts(jnp.where(entry >= 0, returned[k], 0.0))
            entry16 = row_of(send, k, 16)
            chunk = (entry16 >> 7).astype(jnp.float32).astype(jnp.bfloat16)
            place = (entry16 & (LANES - 1)).astype(jnp.float32).astype(jnp.bfloat16)
            lefts.append(
                jnp.concatenate(
                    [jnp.where(chunk == float(i), part, zero16[:16]) for i in range(chunks)],
                    axis=0,
                )
            )
            place = jnp.concatenate([place] * 8, axis=0)
            rights.append(jnp.where(columns == place, one16, zero16))
        total = total + lax.dot_general(
            jnp.concatenate(lefts, axis=1),
            jnp.concatenate(rights, axis=1),
            (((1,), (1,)), ((), ())),
            preferred_element_type=jnp.float32,
        )
    for c in range(chunks):
        out = (
            acc[pl.ds(c * TERM, TERM), :]
            + total[16 * c : 16 * c + 8]
            + total[16 * c + 8 : 16 * c + 16]
        )
        res[:, pl.ds(c * LANES, LANES)] = out[0:6]
        hess[pl.ds(c, 1), :] = out[6:7]


def shards(
    ndev,
    stress,
    stress_dir,
    adjoint,
    relax,
    relax_dir,
    connect,
    mass_mat,
    adv_mat,
    vel_grad,
    send_list,
    elem_count,
):
    nodes = stress.shape[1]
    elems = connect.shape[1]
    chunks = nodes // LANES
    f32, i32 = jnp.float32, jnp.int32

    def by_groups(matrix, rows):
        split = matrix.reshape(-1, rows, elems // LANES, LANES)
        return split.transpose(0, 2, 1, 3).reshape(-1, LANES)

    args = (
        stress,
        stress_dir,
        adjoint,
        relax.reshape(chunks, LANES),
        relax_dir.reshape(chunks, LANES),
        by_groups(connect, 4),
        by_groups(mass_mat, 8),
        by_groups(adv_mat, 8),
        vel_grad,
        send_list.reshape(LISTS, LANES),
        elem_count,
    )
    hbm = pl.BlockSpec(memory_space=pl.ANY)
    acc, returned = pl.pallas_call(
        make_kernel(ndev, nodes, elems),
        out_shape=(
            jax.ShapeDtypeStruct((chunks * TERM, LANES), f32),
            jax.ShapeDtypeStruct((LISTS, TERM, LANES), f32),
        ),
        in_specs=[hbm] * 10 + [pl.BlockSpec(memory_space=pltpu.SMEM)],
        out_specs=(hbm, hbm),
        scratch_shapes=[
            pltpu.VMEM((6, nodes), f32),
            pltpu.VMEM((6, nodes), f32),
            pltpu.VMEM((6, nodes), f32),
            pltpu.VMEM((chunks, LANES), f32),
            pltpu.VMEM((chunks, LANES), f32),
            pltpu.VMEM((elems // 32, LANES), i32),
            pltpu.VMEM((elems // 8, LANES), f32),
            pltpu.VMEM((elems // 8, LANES), f32),
            pltpu.VMEM((9, elems), f32),
            pltpu.VMEM((LISTS, LANES), i32),
            pltpu.VMEM(((chunks + 1) * ROWS, LANES), f32),
            pltpu.VMEM((LISTS, ROWS, LANES), f32),
            pltpu.VMEM((LISTS, ROWS, LANES), f32),
            pltpu.VMEM((2, WIN * ROWS, LANES), f32),
            pltpu.VMEM((2, WIN * ROWS, LANES), f32),
            pltpu.VMEM((20 * WIN, 8, LANES), f32),
            pltpu.VMEM((20 * WIN, 8, LANES), f32),
            pltpu.VMEM((80, 8, LANES), f32),
            pltpu.VMEM((80, 8, LANES), f32),
            pltpu.VMEM((64, LANES), f32),
            pltpu.VMEM((64, LANES), f32),
            pltpu.VMEM((8, LANES), f32),
            pltpu.VMEM((8, LANES), f32),
            pltpu.VMEM((64, LANES), f32),
            pltpu.VMEM((64, LANES), f32),
            pltpu.VMEM((8, LANES), f32),
            pltpu.VMEM((8, LANES), f32),
            pltpu.VMEM((20, 8, LANES), f32),
            pltpu.VMEM((20, 8, LANES), f32),
            pltpu.VMEM((80, 8, LANES), f32),
            pltpu.VMEM((80, 8, LANES), f32),
            pltpu.VMEM((LISTS, 2, 32, LANES), f32),
            pltpu.VMEM((LISTS, 4, 8, LANES), i32),
            pltpu.VMEM((4, 8 * TERM, LANES), f32),
            pltpu.VMEM((4, 8 * TERM, LANES), f32),
            pltpu.VMEM(((chunks + 1) * TERM, LANES), f32),
            pltpu.VMEM((LISTS, TERM, LANES), f32),
            pltpu.SemaphoreType.DMA((10,)),
            pltpu.SemaphoreType.DMA((1,)),
            pltpu.SemaphoreType.DMA((LISTS,)),
            pltpu.SemaphoreType.DMA((LISTS,)),
            pltpu.SemaphoreType.DMA((LISTS,)),
            pltpu.SemaphoreType.DMA((LISTS,)),
        ],
        compiler_params=pltpu.CompilerParams(
            collective_id=0,
            has_side_effects=True,
            vmem_limit_bytes=62 * 1024 * 1024,
        ),
    )(*args)
    res, hess = pl.pallas_call(
        finish,
        out_shape=(
            jax.ShapeDtypeStruct((6, nodes), f32),
            jax.ShapeDtypeStruct((chunks, LANES), f32),
        ),
        compiler_params=pltpu.CompilerParams(vmem_limit_bytes=62 * 1024 * 1024),
    )(acc, returned, args[9])
    return res, hess.reshape(nodes)


def solution(mesh):
    ndev = mesh.shape["dom"]

    def run(*args):
        return shards(ndev, *args)

    return jax.shard_map(
        run,
        mesh=mesh,
        in_specs=(
            P(None, "dom"),
            P(None, "dom"),
            P(None, "dom"),
            P("dom"),
            P("dom"),
            P(None, "dom"),
            P(None, "dom"),
            P(None, "dom"),
            P(None, "dom"),
            P("dom"),
            P("dom"),
        ),
        out_specs=(P(None, "dom"), P("dom")),
        check_vma=False,
    )
```

```python
import jax
import jax.numpy as jnp
from jax import lax
from jax.experimental import pallas as pl
from jax.experimental.pallas import tpu as pltpu
from jax.sharding import PartitionSpec as P

HOPS = 8
LISTS = 2 * HOPS
ELEM_BLOCK = 512
KAPPA = 0.5
PAIRS = ((0, 0), (1, 1), (2, 2), (0, 1), (0, 2), (1, 2))
LAYOUT = ((0, 3, 4), (3, 1, 5), (4, 5, 2))

LANES = 128
ROWS = 24
TAU, LAM, DLAM, DIR, ADJ = 0, 6, 7, 8, 14
FIELDS = 20
FIELD_ROWS = tuple(range(FIELDS))
WIN = 3
TERM = 8

GATHER = lax.GatherDimensionNumbers(
    offset_dims=(),
    collapsed_slice_dims=(1,),
    start_index_map=(1,),
    operand_batching_dims=(0,),
    start_indices_batching_dims=(0,),
)


def pick_lanes(table, lane):
    return lax.gather(
        table,
        lane[:, :, None],
        GATHER,
        slice_sizes=(1, 1),
        mode=lax.GatherScatterMode.PROMISE_IN_BOUNDS,
    )


def list_offset(index):
    return jnp.where(index < HOPS, index + 1, HOPS - 1 - index)


def row_of(ref, row, height=8):
    return jnp.broadcast_to(ref[pl.ds(row, 1), :], (height, LANES))


def two_parts(values):
    high = values.astype(jnp.bfloat16).astype(jnp.float32)
    return jnp.concatenate([high, values - high], axis=0).astype(jnp.bfloat16)


def symmetric_product(left, right):
    prod = [
        [
            left[row][0] * right[LAYOUT[0][col]]
            + left[row][1] * right[LAYOUT[1][col]]
            + left[row][2] * right[LAYOUT[2][col]]
            for col in range(3)
        ]
        for row in range(3)
    ]
    return [prod[row][col] + prod[col][row] for row, col in PAIRS]


def make_kernel(ndev, nodes, elems):
    chunks = nodes // LANES
    nblocks = elems // ELEM_BLOCK
    groups = ELEM_BLOCK // LANES
    span = max(nblocks - 1, 1)
    window = WIN * LANES
    turns = LISTS // 2

    def kernel(
        stress_hbm,
        dir_hbm,
        adj_hbm,
        relax_hbm,
        rdir_hbm,
        conn_hbm,
        mass_hbm,
        adv_hbm,
        grad_hbm,
        send_hbm,
        count_ref,
        acc_hbm,
        returned,
        stress,
        sdir,
        adjoint,
        relax,
        rdir,
        conn,
        mass,
        adv,
        grad,
        send,
        fields,
        payload,
        ghosts,
        rolled0,
        rolled1,
        table0,
        table1,
        owned0,
        owned1,
        owned2,
        vel0,
        vel1,
        vel2,
        vel80,
        vel81,
        vel82,
        mvel0,
        mvel1,
        mvel80,
        mvel81,
        gtable0,
        gtable1,
        merged0,
        merged1,
        index,
        rels,
        terms0,
        terms1,
        acc,
        gout,
        in_sem,
        out_sem,
        send_sem,
        recv_sem,
        back_sem,
        ret_sem,
    ):
        me = lax.axis_index("dom")
        loads = [
            pltpu.make_async_copy(src, dst, in_sem.at[i])
            for i, (src, dst) in enumerate(
                [
                    (stress_hbm, stress),
                    (dir_hbm, sdir),
                    (adj_hbm, adjoint),
                    (relax_hbm, relax),
                    (rdir_hbm, rdir),
                    (send_hbm, send),
                    (conn_hbm, conn),
                    (grad_hbm, grad),
                    (mass_hbm, mass),
                    (adv_hbm, adv),
                ]
            )
        ]
        for load in loads:
            load.start()

        def inside(device):
            return (device >= 0) & (device < ndev)

        barrier = pltpu.get_barrier_semaphore()

        @pl.loop(0, LISTS)
        def _(k):
            target = me + list_offset(k)

            @pl.when(inside(target))
            def _():
                pl.semaphore_signal(
                    barrier, inc=1, device_id=(target,), device_id_type=pl.DeviceIdType.MESH
                )

        zeros = jnp.zeros((8, LANES), jnp.float32)
        lane = lax.broadcasted_iota(jnp.int32, (8, LANES), 1)
        sub = lax.broadcasted_iota(jnp.int32, (8, LANES), 0)
        upper = sub >= groups

        for load in loads[:6]:
            load.wait()

        for c in range(chunks):
            cut = pl.ds(c * LANES, LANES)
            fields[pl.ds(c * ROWS + 16, 8), :] = zeros
            fields[pl.ds(c * ROWS + TAU, 6), :] = 0.5 * KAPPA * stress[:, cut]
            fields[pl.ds(c * ROWS + LAM, 1), :] = relax[pl.ds(c, 1), :]
            fields[pl.ds(c * ROWS + DLAM, 1), :] = rdir[pl.ds(c, 1), :]
            fields[pl.ds(c * ROWS + DIR, 6), :] = sdir[:, cut]
            fields[pl.ds(c * ROWS + ADJ, 6), :] = adjoint[:, cut]
        for base in (0, 8, 16):
            fields[pl.ds(chunks * ROWS + base, 8), :] = zeros

        def starts_of(pair):
            one = (2 * pair) * (nodes - window) // span
            two = (2 * pair + 1) * (nodes - window) // span
            return one, two

        def relative(pair, k):
            one, two = starts_of(pair)
            lists_one = (2 * pair) % LISTS
            node = conn[pl.ds(pair * 32 + k, 8, stride=4), :]
            start = jnp.where(upper, two, one)
            ghost0 = nodes + LANES * jnp.where(upper, lists_one + 1, lists_one) - window
            return node - jnp.where(node >= nodes, ghost0, start)

        count = count_ref[0]
        columns = lax.broadcasted_iota(jnp.int32, (LANES, LANES), 0).astype(jnp.bfloat16)
        one16 = jnp.ones((LANES, LANES), jnp.bfloat16)
        zero16 = jnp.zeros((LANES, LANES), jnp.bfloat16)
        contract = (((1,), (1,)), ((), ()))

        def factor(place_row):
            return jnp.where(columns == place_row, one16, zero16)

        def mark(pair):
            live = (pair * 8 + sub) * LANES + lane < count
            for k in range(4):
                rel = relative(pair, k)
                rels[pair, k] = rel
                index[pair, 0, pl.ds(8 * k, 8), :] = (rel & (LANES - 1)).astype(jnp.float32)
                index[pair, 1, pl.ds(8 * k, 8), :] = jnp.where(live, rel >> 7, -1).astype(
                    jnp.float32
                )

        for load in loads[6:7]:
            load.wait()

        def pick(k):
            entry = row_of(send, k)
            place = entry & (LANES - 1)
            chunk = entry >> 7
            picked = [zeros, zeros, zeros]
            for c in range(chunks):
                here = chunk == c
                for t in range(3):
                    got = pick_lanes(fields[pl.ds(c * ROWS + 8 * t, 8), :], place)
                    picked[t] = jnp.where(here, got, picked[t])
            for t in range(3):
                payload[k, pl.ds(8 * t, 8), :] = picked[t]
            mark(k)

        def push(k):
            target = me + list_offset(k)
            return pltpu.make_async_remote_copy(
                src_ref=payload.at[k, pl.ds(0, FIELDS)],
                dst_ref=ghosts.at[k, pl.ds(0, FIELDS)],
                send_sem=send_sem.at[k],
                recv_sem=recv_sem.at[k],
                device_id=(target,),
                device_id_type=pl.DeviceIdType.MESH,
            )

        def push_back(k):
            target = me - list_offset(k)
            return pltpu.make_async_remote_copy(
                src_ref=gout.at[k],
                dst_ref=returned.at[k],
                send_sem=back_sem.at[k],
                recv_sem=ret_sem.at[k],
                device_id=(target,),
                device_id_type=pl.DeviceIdType.MESH,
            )

        def send_off(k):
            @pl.when(inside(me + list_offset(k)))
            def _():
                push(k).start()

        early = LISTS // 4

        @pl.loop(0, early)
        def _(i):
            pick((i + HOPS) % LISTS)

        pl.semaphore_wait(barrier, jnp.minimum(HOPS, ndev - 1 - me) + jnp.minimum(HOPS, me))

        @pl.loop(0, early)
        def _(i):
            send_off((i + HOPS) % LISTS)

        @pl.loop(early, LISTS)
        def _(i):
            pick((i + HOPS) % LISTS)
            send_off((i + HOPS) % LISTS)

        for i in range(chunks + 1):
            acc[pl.ds(i * TERM, TERM), :] = zeros
        for i in range(LISTS):
            gout[i] = zeros
        for terms in (terms0, terms1):
            for k in range(4):
                for g in range(8):
                    terms[k, pl.ds(g * TERM, TERM), :] = zeros
        loads[7].wait()

        def weave(one, two):
            spent = [0, 0]
            parts = [one, two]
            while parts[0] is not None or parts[1] is not None:
                which = 0 if spent[0] <= spent[1] else 1
                if parts[which] is None:
                    which = 1 - which
                cost = next(parts[which], None)
                if cost is None:
                    parts[which] = None
                else:
                    spent[which] += cost

        def run(*parts):
            for part in parts:
                for _ in part:
                    pass

        def prepare(pair, rolled, table):
            for which, start in enumerate(starts_of(pair)):
                chunk0 = start // LANES
                shift = start % LANES
                keep = lane < LANES - shift
                for t in range(3):
                    turned = [
                        pltpu.roll(
                            fields[
                                pl.ds(pl.multiple_of((chunk0 + i) * ROWS + 8 * t, 8), 8), :
                            ],
                            (LANES - shift) % LANES,
                            1,
                        )
                        for i in range(WIN + 1)
                    ]
                    for i in range(WIN):
                        rolled[which, pl.ds(i * ROWS + 8 * t, 8), :] = jnp.where(
                            keep, turned[i], turned[i + 1]
                        )
            yield 50
            for n, row in enumerate(FIELD_ROWS):
                for i in range(WIN):
                    table[n * WIN + i] = jnp.where(
                        upper,
                        row_of(rolled.at[1], i * ROWS + row),
                        row_of(rolled.at[0], i * ROWS + row),
                    )
            yield 20

        def gather_owned(pair, table, owned, vel, vel8):
            for k in range(4):
                rel = rels[pair, k]
                place = rel & (LANES - 1)
                first = rel < LANES
                second = rel < 2 * LANES
                for n in range(20):
                    a, b, c = [pick_lanes(table[n * WIN + i], place) for i in range(WIN)]
                    owned[k * 20 + n] = jnp.where(first, a, jnp.where(second, b, c))
                    if n % 4 == 3:
                        yield 24
            for j in range(8):
                cut = pl.ds(pl.multiple_of((pair * 8 + j) * LANES, LANES), LANES)
                vel[pl.ds(j * 8, 8), :] = grad[0:8, cut]
                vel8[pl.ds(j, 1), :] = grad[8:9, cut]
            yield 8

        def at_turn(step):
            return (step + turns // 2) % turns

        def await_ghosts(turn):
            for which in range(2):
                k = 2 * turn + which

                @pl.when(inside(me - list_offset(k)))
                def _():
                    push(k).wait_recv()

        first, second, third = at_turn(0), at_turn(1), at_turn(2)
        run(prepare(first, rolled0, table0), prepare(first + turns, rolled1, table1))
        run(gather_owned(first, table0, owned2, vel2, vel82), prepare(second, rolled0, table0))
        run(
            gather_owned(first + turns, table1, owned1, vel1, vel81),
            prepare(second + turns, rolled1, table1),
        )
        run(gather_owned(second, table0, owned0, vel0, vel80), prepare(third, rolled0, table0))

        for load in loads[8:]:
            load.wait()

        def gather_ghosts(pair, gtable, owned, vel_in, vel8_in, merged, vel, vel8):
            listed = (2 * pair) % LISTS
            for n, row in enumerate(FIELD_ROWS):
                gtable[n] = jnp.where(
                    upper, row_of(ghosts.at[listed + 1], row), row_of(ghosts.at[listed], row)
                )
            vel[...] = vel_in[...]
            vel8[...] = vel8_in[...]
            yield 15
            for k in range(4):
                rel = rels[pair, k]
                place = rel & (LANES - 1)
                ghostly = rel >= window
                for n in range(20):
                    merged[k * 20 + n] = jnp.where(
                        ghostly, pick_lanes(gtable[n], place), owned[k * 20 + n]
                    )
                    if n % 10 == 9:
                        yield 20

        def algebra(pair, merged, vel_rows, vel8, terms):
            def got(k, n):
                return merged[k * 20 + n]

            lam_e = 0.25 * (got(0, 6) + got(1, 6) + got(2, 6) + got(3, 6))
            dlam4 = got(0, 7) + got(1, 7) + got(2, 7) + got(3, 7)
            vel = [vel_rows[pl.ds(i, 8, stride=8), :] for i in range(8)] + [vel8[...]]
            tdir, gin, wsum, usum = [], [], [], []
            for k in range(4):
                tau = [got(k, c) for c in range(6)]
                t = [got(k, 8 + c) for c in range(6)]
                left_b = [
                    [tau[LAYOUT[r][c]] - vel[3 * r + c] for c in range(3)] for r in range(3)
                ]
                left_g = [
                    [left_b[r][c] + tau[LAYOUT[r][c]] for c in range(3)] for r in range(3)
                ]
                b_in = symmetric_product(left_b, tau)
                tdir.append(t)
                gin.append(symmetric_product(left_g, t))
                wsum.append([dlam4 * s for s in tau])
                usum.append([t[c] + dlam4 * b_in[c] for c in range(6)])
                yield 38
            score = zeros
            for a in range(4):
                mat, adm = [], []
                for b in range(4):
                    entry = 4 * a + b
                    at = (entry // 8) * (elems // 16) + pair * 64 + entry % 8
                    mat.append(mass[pl.ds(at, 8, stride=8), :])
                    adm.append(adv[pl.ds(at, 8, stride=8), :])
                for c in range(6):
                    g = adm[0] * tdir[0][c] + mat[0] * gin[0][c]
                    d = adm[0] * wsum[0][c] + mat[0] * usum[0][c]
                    for b in range(1, 4):
                        g = g + (adm[b] * tdir[b][c] + mat[b] * gin[b][c])
                        d = d + (adm[b] * wsum[b][c] + mat[b] * usum[b][c])
                    score = score + got(a, 14 + c) * g
                    terms[a, pl.ds(c, 8, stride=TERM), :] = d + lam_e * g
                    if c % 2 == 1:
                        yield 17
            score = 0.25 * score
            for a in range(4):
                terms[a, pl.ds(6, 8, stride=TERM), :] = score
            yield 2

        def scatter(pair, terms):
            listed = (2 * pair) % LISTS
            for which, start in enumerate(starts_of(pair)):
                lefts, rights = [], []
                for k in range(4):
                    for j in range(groups):
                        g = which * groups + j
                        part = two_parts(terms[k, pl.ds(g * TERM, TERM), :])
                        chunk = row_of(index.at[pair, 1], 8 * k + g, 16).astype(jnp.bfloat16)
                        place = row_of(index.at[pair, 0], 8 * k + g, 16).astype(jnp.bfloat16)
                        rights.append(factor(jnp.concatenate([place] * 8, axis=0)))
                        lefts.append(
                            jnp.concatenate(
                                [
                                    jnp.where(chunk == float(i), part, zero16[:16])
                                    for i in range(4)
                                ],
                                axis=0,
                            )
                        )
                    yield 32
                total = lax.dot_general(
                    jnp.concatenate(lefts, axis=1),
                    jnp.concatenate(rights, axis=1),
                    contract,
                    preferred_element_type=jnp.float32,
                )
                sums = [
                    total[16 * i : 16 * i + 8] + total[16 * i + 8 : 16 * i + 16]
                    for i in range(4)
                ]
                chunk0 = start // LANES
                shift = start % LANES
                turned = [pltpu.roll(sums[i], shift, 1) for i in range(WIN)]
                later = lane >= shift
                for i in range(WIN + 1):
                    if i == 0:
                        add = jnp.where(later, turned[0], 0.0)
                    elif i == WIN:
                        add = jnp.where(later, 0.0, turned[WIN - 1])
                    else:
                        add = jnp.where(later, turned[i], turned[i - 1])
                    at = pl.ds(pl.multiple_of((chunk0 + i) * TERM, TERM), TERM)
                    acc[at, :] = acc[at, :] + add
                gout[listed + which] = gout[listed + which] + sums[WIN]
                yield 10

        def both(one, two):
            yield from one
            yield from two

        def give_back(turn):
            for which in range(2):
                k = 2 * turn + which

                @pl.when(inside(me - list_offset(k)))
                def _():
                    push_back(k).start()

        def merge(turn, half):
            if half == 0:
                return gather_ghosts(
                    turn, gtable0, owned0, vel0, vel80, merged0, mvel0, mvel80
                )
            return gather_ghosts(
                turn + turns, gtable1, owned1, vel1, vel81, merged1, mvel1, mvel81
            )

        def look_ahead(turn, after, half):
            if half == 0:
                yield from gather_owned(turn, table0, owned0, vel0, vel80)
                yield from prepare(after, rolled0, table0)
            else:
                yield from gather_owned(turn + turns, table1, owned1, vel1, vel81)
                yield from prepare(after + turns, rolled1, table1)

        await_ghosts(first)
        run(gather_ghosts(first, gtable0, owned2, vel2, vel82, merged0, mvel0, mvel80))

        @pl.loop(0, turns)
        def _(step):
            before = at_turn(jnp.maximum(step - 1, 0))
            turn = at_turn(step)
            one, two, three = [
                at_turn(jnp.minimum(step + ahead, turns - 1)) for ahead in (1, 2, 3)
            ]

            @pl.when(step < turns - 1)
            def _():
                await_ghosts(one)

            weave(
                both(merge(turn, 1), look_ahead(one, two, 1)),
                both(
                    algebra(turn, merged0, mvel0, mvel80, terms0),
                    scatter(before + turns, terms1),
                ),
            )
            weave(
                both(merge(one, 0), look_ahead(two, three, 0)),
                both(
                    algebra(turn + turns, merged1, mvel1, mvel81, terms1),
                    scatter(turn, terms0),
                ),
            )

            @pl.when(step > 0)
            def _():
                give_back(before)

        last = at_turn(turns - 1)
        run(scatter(last + turns, terms1))
        give_back(last)

        store = pltpu.make_async_copy(acc.at[pl.ds(0, chunks * TERM)], acc_hbm, out_sem.at[0])
        store.start()

        @pl.loop(0, LISTS)
        def _(k):
            @pl.when(inside(me + list_offset(k)))
            def _():
                push(k).wait_send()
                push_back(k).wait_recv()

            @pl.when(inside(me - list_offset(k)))
            def _():
                push_back(k).wait_send()

        store.wait()

    return kernel


def finish(acc, returned, send, res, hess):
    chunks = hess.shape[0]
    columns = lax.broadcasted_iota(jnp.int32, (LANES, LANES), 0).astype(jnp.bfloat16)
    one16 = jnp.ones((LANES, LANES), jnp.bfloat16)
    zero16 = jnp.zeros((LANES, LANES), jnp.bfloat16)
    total = jnp.zeros((chunks * 2 * TERM, LANES), jnp.float32)
    for pairing in range(LISTS // 2):
        lefts, rights = [], []
        for k in (2 * pairing, 2 * pairing + 1):
            entry = row_of(send, k)
            part = two_parts(jnp.where(entry >= 0, returned[k], 0.0))
            entry16 = row_of(send, k, 16)
            chunk = (entry16 >> 7).astype(jnp.float32).astype(jnp.bfloat16)
            place = (entry16 & (LANES - 1)).astype(jnp.float32).astype(jnp.bfloat16)
            lefts.append(
                jnp.concatenate(
                    [jnp.where(chunk == float(i), part, zero16[:16]) for i in range(chunks)],
                    axis=0,
                )
            )
            place = jnp.concatenate([place] * 8, axis=0)
            rights.append(jnp.where(columns == place, one16, zero16))
        total = total + lax.dot_general(
            jnp.concatenate(lefts, axis=1),
            jnp.concatenate(rights, axis=1),
            (((1,), (1,)), ((), ())),
            preferred_element_type=jnp.float32,
        )
    for c in range(chunks):
        out = (
            acc[pl.ds(c * TERM, TERM), :]
            + total[16 * c : 16 * c + 8]
            + total[16 * c + 8 : 16 * c + 16]
        )
        res[:, pl.ds(c * LANES, LANES)] = out[0:6]
        hess[pl.ds(c, 1), :] = out[6:7]


def shards(
    ndev,
    stress,
    stress_dir,
    adjoint,
    relax,
    relax_dir,
    connect,
    mass_mat,
    adv_mat,
    vel_grad,
    send_list,
    elem_count,
):
    nodes = stress.shape[1]
    elems = connect.shape[1]
    chunks = nodes // LANES
    f32, i32 = jnp.float32, jnp.int32

    def by_groups(matrix, rows):
        split = matrix.reshape(-1, rows, elems // LANES, LANES)
        return split.transpose(0, 2, 1, 3).reshape(-1, LANES)

    args = (
        stress,
        stress_dir,
        adjoint,
        relax.reshape(chunks, LANES),
        relax_dir.reshape(chunks, LANES),
        by_groups(connect, 4),
        by_groups(mass_mat, 8),
        by_groups(adv_mat, 8),
        vel_grad,
        send_list.reshape(LISTS, LANES),
        elem_count,
    )
    hbm = pl.BlockSpec(memory_space=pl.ANY)
    acc, returned = pl.pallas_call(
        make_kernel(ndev, nodes, elems),
        out_shape=(
            jax.ShapeDtypeStruct((chunks * TERM, LANES), f32),
            jax.ShapeDtypeStruct((LISTS, TERM, LANES), f32),
        ),
        in_specs=[hbm] * 10 + [pl.BlockSpec(memory_space=pltpu.SMEM)],
        out_specs=(hbm, hbm),
        scratch_shapes=[
            pltpu.VMEM((6, nodes), f32),
            pltpu.VMEM((6, nodes), f32),
            pltpu.VMEM((6, nodes), f32),
            pltpu.VMEM((chunks, LANES), f32),
            pltpu.VMEM((chunks, LANES), f32),
            pltpu.VMEM((elems // 32, LANES), i32),
            pltpu.VMEM((elems // 8, LANES), f32),
            pltpu.VMEM((elems // 8, LANES), f32),
            pltpu.VMEM((9, elems), f32),
            pltpu.VMEM((LISTS, LANES), i32),
            pltpu.VMEM(((chunks + 1) * ROWS, LANES), f32),
            pltpu.VMEM((LISTS, ROWS, LANES), f32),
            pltpu.VMEM((LISTS, ROWS, LANES), f32),
            pltpu.VMEM((2, WIN * ROWS, LANES), f32),
            pltpu.VMEM((2, WIN * ROWS, LANES), f32),
            pltpu.VMEM((20 * WIN, 8, LANES), f32),
            pltpu.VMEM((20 * WIN, 8, LANES), f32),
            pltpu.VMEM((80, 8, LANES), f32),
            pltpu.VMEM((80, 8, LANES), f32),
            pltpu.VMEM((80, 8, LANES), f32),
            pltpu.VMEM((64, LANES), f32),
            pltpu.VMEM((64, LANES), f32),
            pltpu.VMEM((64, LANES), f32),
            pltpu.VMEM((8, LANES), f32),
            pltpu.VMEM((8, LANES), f32),
            pltpu.VMEM((8, LANES), f32),
            pltpu.VMEM((64, LANES), f32),
            pltpu.VMEM((64, LANES), f32),
            pltpu.VMEM((8, LANES), f32),
            pltpu.VMEM((8, LANES), f32),
            pltpu.VMEM((20, 8, LANES), f32),
            pltpu.VMEM((20, 8, LANES), f32),
            pltpu.VMEM((80, 8, LANES), f32),
            pltpu.VMEM((80, 8, LANES), f32),
            pltpu.VMEM((LISTS, 2, 32, LANES), f32),
            pltpu.VMEM((LISTS, 4, 8, LANES), i32),
            pltpu.VMEM((4, 8 * TERM, LANES), f32),
            pltpu.VMEM((4, 8 * TERM, LANES), f32),
            pltpu.VMEM(((chunks + 1) * TERM, LANES), f32),
            pltpu.VMEM((LISTS, TERM, LANES), f32),
            pltpu.SemaphoreType.DMA((10,)),
            pltpu.SemaphoreType.DMA((1,)),
            pltpu.SemaphoreType.DMA((LISTS,)),
            pltpu.SemaphoreType.DMA((LISTS,)),
            pltpu.SemaphoreType.DMA((LISTS,)),
            pltpu.SemaphoreType.DMA((LISTS,)),
        ],
        compiler_params=pltpu.CompilerParams(
            collective_id=0,
            has_side_effects=True,
            vmem_limit_bytes=62 * 1024 * 1024,
        ),
    )(*args)
    res, hess = pl.pallas_call(
        finish,
        out_shape=(
            jax.ShapeDtypeStruct((6, nodes), f32),
            jax.ShapeDtypeStruct((chunks, LANES), f32),
        ),
        compiler_params=pltpu.CompilerParams(vmem_limit_bytes=62 * 1024 * 1024),
    )(acc, returned, args[9])
    return res, hess.reshape(nodes)


def solution(mesh):
    ndev = mesh.shape["dom"]

    def run(*args):
        return shards(ndev, *args)

    return jax.shard_map(
        run,
        mesh=mesh,
        in_specs=(
            P(None, "dom"),
            P(None, "dom"),
            P(None, "dom"),
            P("dom"),
            P("dom"),
            P(None, "dom"),
            P(None, "dom"),
            P(None, "dom"),
            P(None, "dom"),
            P("dom"),
            P("dom"),
        ),
        out_specs=(P(None, "dom"), P("dom")),
        check_vma=False,
    )
```
